32 devices in a mesh: dp: 8 (over y, x, core), expert: 4 (over z).
Axes of the slice: x: 2, y: 2, z: 4, core: 2. Of those that a mesh axis runs over, the one named last changes fastest.
Arguments:
- tokens_in: bfloat16 [8192, 2048], P(('dp', 'expert')), may hold values from -6 to 6
- out_grad: bfloat16 [8192, 2048], P(('dp', 'expert')), may hold values from -6 to 6
- expert_ids: int32 [8192, 2], P(('dp', 'expert')), may hold values from 0 to 3, all different within a row; in each aligned block of 256 rows (0 to 255, 256 to 511, ...) at most 160 rows name the same one
- gate_weights: float32 [8192, 2], P(('dp', 'expert')), may hold values from 0.05 to 0.5
- w_gate_up: bfloat16 [4, 2048, 1536], P('expert'), may hold values from -0.125 to 0.125
- w_down: bfloat16 [4, 768, 2048], P('expert'), may hold values from -0.21875 to 0.21875
Outputs:
- grad_tokens: bfloat16 [8192, 2048], P(('dp', 'expert'))
- grad_gate_up: float32 [2048, 6144], P('dp', 'expert')
- grad_down: float32 [768, 8192], P('dp', 'expert')
The draws below stay inside these ranges and needn't reach their ends.
Inputs may be any that keep to these rules, and one draw needn't show every extreme that they name: `expert_ids`: each row names 2 different experts; every expert is named somewhere. Among the 256 rows of one device (aligned blocks, in order) no expert is named more than 160 times, and in every draw some expert is named exactly 160 times in some block.
All inputs are finite; a program needn't handle non-finite values.
Results may differ from the reference program's by a relative error of at most 0.015.
Values may be sent and summed in bfloat16 or wider, within the bound.
No kernel may reach another device: no remote copies, remote signals or barrier semaphores. Data moves between devices by JAX's collectives and lax.ppermute only.
A program may use at most 128 MiB of HBM per device.

```python
import math
import jax
import jax.numpy as jnp
import numpy as np
from jax import lax

D = 2048
FF = 768
TOPK = 2
TOK_DEV = 256
EXPERTS = 4
CAP = 160
TOKENS = 8192


def with_spikes(drawn, rng, source, target, blocks, factor):
    def block_of(dim):
        return (jnp.arange(drawn.shape[dim]) // (drawn.shape[dim] // blocks)).reshape((-1,) + (1,) * (drawn.ndim - 1 - dim))

    one_side = jax.random.permutation(rng, blocks)[block_of(target)]
    other_side = (block_of(target) + blocks // 2) % blocks
    return jnp.where((block_of(source) == one_side) | (block_of(source) == other_side), factor * drawn, drawn)


def steps_of(rng, extent, split, least, largest):
    gain, own = 1.0, jax.random.fold_in(rng, 6)
    for axis_at, parts in split:
        heights = jnp.exp(jax.random.uniform(jax.random.fold_in(own, axis_at), (parts,), jnp.float32, least / len(split), largest / len(split)))
        gain = gain * jnp.repeat(heights, extent[axis_at] // parts).reshape([-1 if axis == axis_at else 1 for axis in range(len(extent))])
    return gain


def shared_out(stream_key, own, number, rows, number_of, top, reach, slope):
    order = jax.random.permutation(stream_key, number_of)
    crowded, common = shares(number_of, rows * top, reach, slope, True), shares(number_of, rows * top, reach, slope, False)
    places = jnp.arange(number_of)

    def named(sizes, rotation):
        used = int((sizes > 0).sum())
        fixed = max(1, used // 4)
        shifted = fixed + (places - fixed + rotation * (used - fixed)) % max(1, number_of - fixed)
        return jnp.zeros((number_of,), jnp.int32).at[order[jnp.where(places < fixed, places, shifted)]].set(jnp.asarray(sizes, jnp.int32))

    sizes = jnp.where(number % 4 == 0, named(crowded, number // 4), named(common, number - number // 4 - 1))
    mixed = jax.random.permutation(jax.random.fold_in(own, 3), number_of)
    donor, taker = mixed[0:number_of // 2 * 2:2], mixed[1:number_of // 2 * 2:2]
    margin = jnp.minimum(sizes[donor] - 1, reach - sizes[taker]) // 2
    margin = jnp.where((donor == order[0]) | (taker == order[0]) | (sizes[taker] == 0), 0, jnp.maximum(margin, 0))
    shifted = jax.random.randint(jax.random.fold_in(own, 4), (number_of // 2,), 0, 1 << 20) % (margin + 1)
    sizes = sizes.at[donor].add(-shifted).at[taker].add(shifted)
    members = jnp.searchsorted(jnp.cumsum(sizes), jnp.arange(rows * top), side="right").astype(jnp.int32)
    listing = members.reshape(top, rows).T
    listing = listing[jax.random.permutation(jax.random.fold_in(own, 1), rows)]
    rotation = jax.random.randint(jax.random.fold_in(own, 2), (rows, 1), 0, top)
    return jnp.take_along_axis(listing, (jnp.arange(top)[None, :] + rotation) % top, axis=1)


def shares(amount, total, reach, slope, full):
    loads = [(1 << 20) // math.isqrt(standing ** slope) + 1 for standing in range(1, amount + 1)]
    largest = reach if full else min(reach, max(-(-total // amount), total * loads[0] // sum(loads)))
    least = 1 if total - largest >= amount - 1 else 0
    given, surplus = [largest] + [least] * (amount - 1), total - largest - least * (amount - 1)
    while surplus > 0:
        free = [i for i in range(1, amount) if given[i] < largest] or [i for i in range(1, amount) if given[i] < reach]
        mass, remaining = sum([loads[i] for i in free]), surplus
        for i in free:
            addition = min(reach - given[i], max(1, remaining * loads[i] // mass), surplus)
            given[i] = given[i] + addition
            surplus = surplus - addition
    return np.array(given)


def noise(key, shape, width, reach, pieces=(), kind=jnp.bfloat16):
    factor_of = steps_of(key, shape, pieces, -0.22, 0.18) if pieces else 1.0
    result = jax.random.normal(key, shape, jnp.float32) * width * factor_of
    return jnp.minimum(jnp.maximum(result, -reach), reach).astype(kind)


def bell_draw_with(own_key, dims, spread, reach, split, heavy, held_as=jnp.bfloat16):
    array = spread * jax.random.normal(own_key, dims, jnp.float32)
    if split:
        array = array * steps_of(own_key, dims, split, -0.22, 0.18)
    return jnp.clip(with_spikes(array, jax.random.fold_in(own_key, 3), *heavy), -reach, reach).astype(held_as)


def setup_inputs(seed: int = 0) -> dict:
    keys = jax.random.split(jax.random.key(seed), 7)
    tokens_in = bell_draw_with(keys[0], (TOKENS, D), 1.0, 6.0, ((0, 32),), (0, 1, 32, 2.75))
    out_grad = noise(keys[1], (TOKENS, D), 1.0, 6.0, ((0, 32),))
    expert_ids_keys = jax.random.split(jax.random.fold_in(keys[2], 1), TOKENS // TOK_DEV)
    expert_ids_turns = jax.random.permutation(jax.random.fold_in(keys[2], 3), TOKENS // TOK_DEV)
    expert_ids = jax.vmap(lambda own, number: shared_out(jax.random.fold_in(keys[2], 2), own, number, TOK_DEV, EXPERTS, TOPK, CAP, 1))(expert_ids_keys, expert_ids_turns).reshape((TOKENS, TOPK))
    gate_weights = jnp.clip(jnp.exp(math.log(0.5) - 2.3025851 * jax.random.uniform(keys[3], (TOKENS, TOPK), jnp.float32) ** steps_of(keys[3], (TOKENS, TOPK), ((0, 32),), -0.2, 0.2)), 0.05, 0.5)
    w_gate_up = noise(keys[4], (EXPERTS, D, 2 * FF), D ** -0.5, 0.125, ((0, 4),))
    w_down = noise(keys[5], (EXPERTS, FF, D), FF ** -0.5, 0.21875, ((0, 4),))
    return dict(tokens_in=tokens_in, out_grad=out_grad, expert_ids=expert_ids, gate_weights=gate_weights, w_gate_up=w_gate_up, w_down=w_down)


def expert_pass(inputs_rows, grad_rows, gate_up, down_weight):
    hidden_units = down_weight.shape[0]
    pre_act = jnp.dot(inputs_rows, gate_up, preferred_element_type=jnp.float32)
    gate_pre = pre_act[:, :hidden_units]
    up_pre = pre_act[:, hidden_units:]
    sigmoid_gate = jax.nn.sigmoid(gate_pre)
    swish_gate = gate_pre * sigmoid_gate
    hidden = (swish_gate * up_pre).astype(jnp.bfloat16)
    grad_hidden = jnp.dot(grad_rows, down_weight.T, preferred_element_type=jnp.float32)
    grad_gate = grad_hidden * up_pre * sigmoid_gate * (1.0 + gate_pre * (1.0 - sigmoid_gate))
    grad_up = grad_hidden * swish_gate
    grad_pre = jnp.concatenate([grad_gate, grad_up], axis=1).astype(jnp.bfloat16)
    back_rows = jnp.dot(grad_pre, gate_up.T, preferred_element_type=jnp.float32).astype(jnp.bfloat16)
    grad_pair = jnp.dot(inputs_rows.T, grad_pre, preferred_element_type=jnp.float32)
    grad_lower = jnp.dot(hidden.T, grad_rows, preferred_element_type=jnp.float32)
    return back_rows, grad_pair, grad_lower


def reference(tokens_in, out_grad, expert_ids, gate_weights, w_gate_up, w_down):
    blocks_total = TOKENS // TOK_DEV
    block_ids = expert_ids.reshape(blocks_total, TOK_DEV * TOPK).astype(jnp.int32)
    one_hot = (block_ids[:, :, None] == jnp.arange(EXPERTS, dtype=jnp.int32)[None, None, :]).astype(jnp.int32)
    position = jnp.sum((jnp.cumsum(one_hot, axis=1) - 1) * one_hot, axis=2).astype(jnp.int32)
    block_base = (jnp.arange(blocks_total, dtype=jnp.int32) * CAP)[:, None]
    slot_index = (block_ids * (blocks_total * CAP) + block_base + position).reshape(-1).astype(jnp.int32)
    slot_total = EXPERTS * blocks_total * CAP
    scaled = (gate_weights[:, :, None] * out_grad[:, None, :].astype(jnp.float32)).astype(jnp.bfloat16).reshape(-1, D)
    repeated = jnp.repeat(tokens_in, TOPK, axis=0)
    blank_rows = jnp.zeros((slot_total, D), tokens_in.dtype)
    inputs_rows = blank_rows.at[slot_index].set(repeated).reshape(EXPERTS, blocks_total * CAP, D)
    grad_rows = blank_rows.astype(scaled.dtype).at[slot_index].set(scaled).reshape(EXPERTS, blocks_total * CAP, D)

    def per_expert(operands):
        return expert_pass(operands[0], operands[1], operands[2], operands[3])

    back_rows, grad_pair, grad_lower = lax.map(per_expert, (inputs_rows, grad_rows, w_gate_up, w_down))
    picked = back_rows.reshape(slot_total, D)[slot_index].reshape(TOKENS, TOPK, D).astype(jnp.float32)
    grad_tokens = jnp.sum(picked, axis=1).astype(jnp.bfloat16)
    grad_gate_up = jnp.transpose(grad_pair, (1, 0, 2)).reshape(D, EXPERTS * 2 * FF)
    grad_down = jnp.transpose(grad_lower, (1, 0, 2)).reshape(FF, EXPERTS * D)
    return grad_tokens, grad_gate_up, grad_down
```

```python
import functools
import math

import jax
import jax.numpy as jnp
from jax import lax
from jax.experimental import pallas as pl
from jax.experimental.pallas import tpu as pltpu
from jax.sharding import PartitionSpec as P

F32 = jnp.float32
BF16 = jnp.bfloat16
MIB = 1024 * 1024


def params(grid_rank, mebibytes):
    return pltpu.CompilerParams(
        dimension_semantics=("arbitrary",) * grid_rank, vmem_limit_bytes=mebibytes * MIB
    )


FREE = pl.CostEstimate(flops=1, bytes_accessed=1, transcendentals=0)


def whole(array):
    rank = array.ndim
    return pl.BlockSpec(
        array.shape, lambda *at: (0,) * rank, pipeline_mode=pl.Buffered(buffer_count=1)
    )


def dot(a, b):
    return lax.dot_general(a, b, (((1,), (0,)), ((), ())), preferred_element_type=F32)


def dot_nt(a, b):
    return lax.dot_general(a, b, (((1,), (1,)), ((), ())), preferred_element_type=F32)


def pick_matrices(me, ids, offsets, capacity):
    top, rows = ids.shape
    lines = max(8, max(offsets) + 1)
    wanted = (lax.broadcasted_iota(jnp.int32, (lines, rows), 0) ^ me).astype(F32)
    named = ids[0:1, :] == wanted
    for k in range(1, top):
        named = named | (ids[k : k + 1, :] == wanted)
    named = named.astype(F32)
    before = lax.broadcasted_iota(jnp.int32, (rows, rows), 0) <= lax.broadcasted_iota(
        jnp.int32, (rows, rows), 1
    )
    place = dot(named.astype(BF16), before.astype(F32).astype(BF16))
    place = jnp.where(named > 0, place - 1.0, -1.0)
    slots = lax.broadcasted_iota(jnp.int32, (capacity, rows), 0).astype(F32)
    return [(place[m : m + 1, :] == slots).astype(F32) for m in offsets]


def pack_kernel(offsets, joint, me_ref, meta_ref, tokens_ref, grads_ref, *rest):
    outs, pick, gain = rest[:-2], rest[-2], rest[-1]
    capacity = pick.shape[1]

    @pl.when(pl.program_id(0) == 0)
    def _():
        me, meta = me_ref[0], meta_ref[...]
        top = meta.shape[0] // 2
        ids, gates = meta[:top], meta[top:]
        for at, matrix in enumerate(pick_matrices(me, ids, offsets, capacity)):
            pick[at] = matrix.astype(BF16)
            chosen = jnp.where(ids == (me ^ offsets[at]).astype(F32), gates, 0.0)
            weight = jnp.sum(chosen, axis=0, keepdims=True)
            gain[at] = jnp.broadcast_to(
                jnp.sum(matrix * weight, axis=1, keepdims=True), gain.shape[1:]
            )

    outs = list(outs)
    for at, m in enumerate(offsets):
        row = dot(pick[at], tokens_ref[...]).astype(BF16)
        grad = (dot(pick[at], grads_ref[...]) * gain[at][:, 0:1]).astype(BF16)
        if m in joint:
            out = outs.pop(0)
            out[0], out[1] = row, grad
        else:
            outs.pop(0)[...] = row
            outs.pop(0)[...] = grad


def pack(me, meta, tokens, grads, offsets, joint, capacity):
    rows, width = tokens.shape
    block = min(width, 512)
    out_specs, out_shape = [], []
    for m in offsets:
        if m in joint:
            out_specs.append(pl.BlockSpec((2, capacity, block), lambda i: (0, 0, i)))
            out_shape.append(jax.ShapeDtypeStruct((2, capacity, width), BF16))
        else:
            out_specs += [pl.BlockSpec((capacity, block), lambda i: (0, i))] * 2
            out_shape += [jax.ShapeDtypeStruct((capacity, width), BF16)] * 2
    count = len(offsets)
    return pl.pallas_call(
        functools.partial(pack_kernel, offsets, joint),
        grid=(width // block,),
        in_specs=[
            pl.BlockSpec(memory_space=pltpu.SMEM),
            pl.BlockSpec(meta.shape, lambda i: (0, 0)),
            pl.BlockSpec((rows, block), lambda i: (0, i)),
            pl.BlockSpec((rows, block), lambda i: (0, i)),
        ],
        out_specs=out_specs,
        out_shape=out_shape,
        scratch_shapes=[
            pltpu.VMEM((count, capacity, rows), BF16),
            pltpu.VMEM((count, capacity, 128), F32),
        ],
        compiler_params=params(1, 14),
        cost_estimate=FREE,
        name="pack",
    )(me, meta, tokens, grads)


def combine_kernel(group, me_ref, meta_ref, *refs):
    blocks, out, pick = refs[:group], refs[group], refs[group + 1]
    capacity = blocks[0].shape[0]

    @pl.when(pl.program_id(0) == 0)
    def _():
        ids = meta_ref[...][: meta_ref.shape[0] // 2]
        matrices = pick_matrices(me_ref[0], ids, list(range(group)), capacity)
        for m, matrix in enumerate(matrices):
            pick[m] = matrix.T.astype(BF16)

    total = dot(pick[0], blocks[0][...])
    for m in range(1, group):
        total += dot(pick[m], blocks[m][...])
    out[...] = total.astype(BF16)


def combine(me, meta, blocks):
    group, (capacity, width) = len(blocks), blocks[0].shape
    rows = meta.shape[1]
    block = min(width, 512)
    return pl.pallas_call(
        functools.partial(combine_kernel, group),
        grid=(width // block,),
        in_specs=[
            pl.BlockSpec(memory_space=pltpu.SMEM),
            pl.BlockSpec(meta.shape, lambda i: (0, 0)),
        ]
        + [pl.BlockSpec((capacity, block), lambda i: (0, i))] * group,
        out_specs=pl.BlockSpec((rows, block), lambda i: (0, i)),
        out_shape=jax.ShapeDtypeStruct((rows, width), BF16),
        scratch_shapes=[pltpu.VMEM((group, rows, capacity), BF16)],
        compiler_params=params(1, 10),
        cost_estimate=FREE,
        name="combine",
    )(me, meta, *blocks)


def padded(rows):
    return -(-rows // 128) * 128


def gather_rows(parts, sizes, held):
    at, parts = 0, list(parts)
    for size in sizes:
        mine, parts = parts[:size], parts[size:]
        rows = mine[0][...]
        for other in mine[1:]:
            rows = rows + other[...]
        held[at : at + rows.shape[0], :] = rows
        at += rows.shape[0]
    if at < held.shape[0]:
        held[at:, :] = jnp.zeros((held.shape[0] - at, held.shape[1]), held.dtype)


def part_spec(array, capacity, which):
    width = array.shape[-1]
    once = pl.Buffered(buffer_count=1)
    if array.ndim == 2:
        return pl.BlockSpec((capacity, width), lambda i: (0, 0), pipeline_mode=once)
    return pl.BlockSpec((None, capacity, width), lambda i: (which, 0, 0), pipeline_mode=once)


def forward_kernel(sizes, *refs):
    count = sum(sizes)
    gate_w, up_w = refs[count : count + 2]
    gate_out, up_out, hidden_out, flipped, held = refs[-5:]

    @pl.when(pl.program_id(0) == 0)
    def _():
        gather_rows(refs[:count], sizes, held)
        step = min(held.shape[1], 256)
        for d in range(0, held.shape[1], step):
            flipped[d : d + step, :] = held[:, d : d + step].T

    gate, up = dot(held[...], gate_w[...]), dot(held[...], up_w[...])
    sigmoid = jax.nn.sigmoid(gate)
    swish = gate * sigmoid
    gate_out[...] = (up * sigmoid * (1.0 + gate * (1.0 - sigmoid))).astype(BF16)
    up_out[...] = swish.astype(BF16)
    hidden_out[...] = (swish * up).T.astype(BF16)


def forward(half, sources, w_pair, before):
    arrays, sizes = sum(sources, []), [len(s) for s in sources]
    capacity, width = arrays[0].shape[-2:]
    units = w_pair.shape[1] // 2
    tile = math.gcd(units, 256)
    tiles = units // tile
    rows = padded(len(sources) * capacity)
    shapes = [
        jax.ShapeDtypeStruct((rows, units), BF16),
        jax.ShapeDtypeStruct((rows, units), BF16),
        jax.ShapeDtypeStruct((units, 2 * rows), BF16),
        jax.ShapeDtypeStruct((width, 2 * rows), BF16),
    ]
    first = len(arrays) + 2
    return pl.pallas_call(
        functools.partial(forward_kernel, sizes),
        grid=(tiles,),
        in_specs=[part_spec(a, capacity, 0) for a in arrays]
        + [
            pl.BlockSpec((width, tile), lambda j: (0, j)),
            pl.BlockSpec((width, tile), lambda j: (0, tiles + j)),
        ]
        + [pl.BlockSpec(memory_space=pl.ANY) for _ in before],
        out_specs=[
            pl.BlockSpec((rows, tile), lambda j: (0, j)),
            pl.BlockSpec((rows, tile), lambda j: (0, j)),
            pl.BlockSpec((tile, rows), lambda j: (j, half)),
            pl.BlockSpec((width, rows), lambda j: (0, half)),
        ],
        out_shape=shapes,
        scratch_shapes=[pltpu.VMEM((rows, width), BF16)],
        input_output_aliases={first + i: 2 + i for i in range(len(before))},
        compiler_params=params(1, 20),
        cost_estimate=FREE,
        name="forward",
    )(*arrays, w_pair, w_pair, *before)


def inner_kernel(sizes, tiles, rows, *refs):
    count, sources = sum(sizes), len(sizes)
    down_w, gate_d, up_d, w_ref = refs[count : count + 4]
    outs, (grads, gate_out, up_out, grad_pre) = refs[-4 - sources : -4], refs[-4:]
    step = pl.program_id(0)
    units = grad_pre.shape[1] // 2

    @pl.when(step == 0)
    def _():
        gather_rows(refs[:count], sizes, grads)

    for j in range(tiles):

        @pl.when(step == j)
        def _():
            grad_hidden = dot_nt(grads[:rows, :], down_w[...])
            tile = grad_hidden.shape[1]
            for at, slope, out in ((0, gate_d, gate_out), (units, up_d, up_out)):
                value = (grad_hidden * slope[:rows, :].astype(F32)).astype(BF16)
                grad_pre[:, at + j * tile : at + (j + 1) * tile] = value
                out[:rows, :] = value
                if rows < out.shape[0]:
                    out[rows:, :] = jnp.zeros((out.shape[0] - rows, tile), BF16)

    @pl.when(step >= tiles)
    def _():
        back = dot_nt(grad_pre[...], w_ref[...])
        capacity = rows // sources
        for m, out in enumerate(outs):
            out[...] = back[m * capacity : (m + 1) * capacity, :].astype(BF16)


def inner(half, sources, w_down, gate_d, up_d, w_pair, before):
    arrays, sizes = sum(sources, []), [len(s) for s in sources]
    capacity, width = arrays[0].shape[-2:]
    units = w_down.shape[0]
    tile = math.gcd(units, 256)
    tiles = units // tile
    block = min(width, 512)
    rows = len(sources) * capacity
    held = padded(rows)

    def tile_at(i):
        return jnp.minimum(i, tiles - 1)

    def block_at(i):
        return jnp.maximum(i - tiles, 0)

    first, outs = len(arrays) + 4, len(sources)
    return pl.pallas_call(
        functools.partial(inner_kernel, sizes, tiles, rows),
        grid=(tiles + width // block,),
        in_specs=[part_spec(a, capacity, 1) for a in arrays]
        + [
            pl.BlockSpec((tile, width), lambda i: (tile_at(i), 0)),
            pl.BlockSpec((held, tile), lambda i: (0, tile_at(i))),
            pl.BlockSpec((held, tile), lambda i: (0, tile_at(i))),
            pl.BlockSpec((block, 2 * units), lambda i: (block_at(i), 0)),
        ]
        + [pl.BlockSpec(memory_space=pl.ANY) for _ in before],
        out_specs=[pl.BlockSpec((capacity, block), lambda i: (0, block_at(i)))] * outs
        + [
            pl.BlockSpec((held, width), lambda i: (half, 0)),
            pl.BlockSpec((held, tile), lambda i: (half, tile_at(i))),
            pl.BlockSpec((held, tile), lambda i: (half, tile_at(i))),
        ],
        out_shape=[jax.ShapeDtypeStruct((capacity, width), BF16)] * outs
        + [
            jax.ShapeDtypeStruct((2 * held, width), BF16),
            jax.ShapeDtypeStruct((2 * held, units), BF16),
            jax.ShapeDtypeStruct((2 * held, units), BF16),
        ],
        scratch_shapes=[pltpu.VMEM((rows, 2 * units), BF16)],
        input_output_aliases={first + i: outs + i for i in range(len(before))},
        compiler_params=params(1, 20),
        cost_estimate=FREE,
        name="inner",
    )(*arrays, w_down, gate_d, up_d, w_pair, *before)


def pair_chunks(flipped_rows, sides, chunk):
    for side in sides:
        for c in range(0, side.shape[1], chunk):
            yield dot(flipped_rows, side[:, c : c + chunk])


def lower_share(rows, chunk):
    return jnp.concatenate([rows[:, c : c + chunk] for c in range(0, rows.shape[1], chunk)], axis=0)


def hold_lower(which, shares, hidden_ref, rows, lower):
    own = hidden_ref.shape[1]
    stacked = jnp.concatenate(
        [hidden_ref[which(r)].astype(F32) for r in range(shares)], axis=0
    ).astype(BF16)
    lower[...] = dot(stacked, rows).reshape(shares, own, rows.shape[1])


def give_kernel(shares, chunk, which_ref, flip_ref, hidden_ref, grads, gate, up, out, lower):
    step = pl.program_id(0)

    @pl.when(step == 0)
    def _():
        hold_lower(lambda r: which_ref[r], shares, hidden_ref, grads[...], lower)

    at = 0
    for piece in pair_chunks(flip_ref[0], (gate[...], up[...]), chunk):
        out[0, at : at + piece.shape[0]] = piece.astype(BF16)
        at += piece.shape[0]
    out[0, at:] = lower_share(lower[step], chunk).astype(BF16)


def shared_operands(flipped, hidden, replicas):
    width, rows = flipped.shape
    units = hidden.shape[0]
    return (
        flipped.reshape(replicas, width // replicas, rows),
        hidden.reshape(replicas, units // replicas, rows),
    )


def give(which, flipped, hidden, grads, gate, up, replicas, chunk):
    rows, width = grads.shape
    units = gate.shape[1]
    shares = replicas // 2
    share_rows = (2 * units * (width // replicas) + (units // replicas) * width) // chunk
    flipped, hidden = shared_operands(flipped, hidden, replicas)
    return pl.pallas_call(
        functools.partial(give_kernel, shares, chunk),
        grid_spec=pltpu.PrefetchScalarGridSpec(
            num_scalar_prefetch=1,
            grid=(shares,),
            in_specs=[pl.BlockSpec((1, width // replicas, rows), lambda i, w: (w[i], 0, 0))]
            + [whole(a) for a in (hidden, grads, gate, up)],
            out_specs=pl.BlockSpec((1, share_rows, chunk), lambda i, w: (i, 0, 0)),
            scratch_shapes=[pltpu.VMEM((shares, units // replicas, width), F32)],
        ),
        out_shape=jax.ShapeDtypeStruct((shares, share_rows, chunk), BF16),
        compiler_params=params(1, 18),
        cost_estimate=FREE,
        name="give",
    )(which, flipped, hidden, grads, gate, up)


def split_kernel(kinds, plan_ref, own, came, *outs):
    step = pl.program_id(0)
    total = own[0].astype(F32) + came[0].astype(F32)
    half = total.shape[0] // 2

    def emit(first, second):
        first[0] = total[:half].astype(BF16)
        second[0] = total[half:].astype(BF16)

    for kind in sorted(set(kinds)):
        chosen = [step == i for i, other in enumerate(kinds) if other == kind]
        pl.when(functools.reduce(jnp.logical_or, chosen))(
            functools.partial(emit, outs[kind[0]], outs[2 + kind[1]])
        )


def without(bits, dropped, r):
    return sum(((r >> bit) & 1) << at for at, bit in enumerate(b for b in bits if b != dropped))


def split(own, came, first_bit, second_bit):
    shares, share_rows, chunk = came.shape
    half = share_rows // 2
    bits = range(shares.bit_length() - 1)

    def kind(r):
        return ((r >> first_bit) & 1, (r >> second_bit) & 1)

    order = sorted(range(shares), key=lambda r: (kind(r), r), reverse=True)
    plan = [order]
    for which, bit in ((0, first_bit), (1, second_bit)):
        for side in (0, 1):
            places = [without(bits, bit, r) if kind(r)[which] == side else None for r in order]
            last = next(p for p in places if p is not None)
            held = []
            for place in places:
                last = last if place is None else place
                held.append(last)
            plan.append(held)
    share = pl.BlockSpec((1, share_rows, chunk), lambda i, p: (p[0, i], 0, 0))
    return pl.pallas_call(
        functools.partial(split_kernel, [kind(r) for r in order]),
        grid_spec=pltpu.PrefetchScalarGridSpec(
            num_scalar_prefetch=1,
            grid=(shares,),
            in_specs=[share, share],
            out_specs=[
                pl.BlockSpec((1, half, chunk), lambda i, p, n=n: (p[n, i], 0, 0))
                for n in range(1, 5)
            ],
        ),
        out_shape=[jax.ShapeDtypeStruct((shares // 2, half, chunk), BF16)] * 4,
        compiler_params=params(1, 14),
        cost_estimate=FREE,
        name="split",
    )(jnp.asarray(plan, jnp.int32), own, came)


def halvings(kept, sent, bits):
    present = sorted(bits, reverse=True)
    rest = [bit for bit in present if bit != bits[0]]
    tail = kept.shape[1:]
    terms = [(kept.reshape((2,) * len(rest) + tail), rest)]
    done = set()
    for bit in bits:
        if bit == bits[0]:
            give, left = sent.reshape((2,) * len(rest) + tail), rest
        else:
            left = [other for other in present if other not in done and other != bit]
            parts = []
            for array, axes in terms:
                index = tuple(1 if b == bit else 0 if b in done else slice(None) for b in axes)
                parts.append(array[index].astype(F32))
            give = sum(parts).astype(BF16)
        pairs = [(i, i ^ (2 << bit)) for i in range(lax.axis_size("dp"))]
        terms.append((lax.ppermute(give, "dp", pairs), left))
        done.add(bit)
    return [array for array, _ in terms]


def finish_kernel(count, chunk, *refs):
    halves, (pair, lower) = (refs[:count], refs[count : 2 * count]), refs[2 * count :]
    totals = []
    for terms in halves:
        total = terms[0][...].astype(F32)
        for term in terms[1:]:
            total += term[...].astype(F32)
        totals.append(total)
    half = totals[0].shape[0]
    at = 0
    for out in (pair, lower):
        rows, columns = out.shape
        for c in range(0, columns, chunk):
            cut = min(max(half - at, 0), rows)
            if cut:
                out[:cut, c : c + chunk] = totals[0][at : at + cut]
            if cut < rows:
                out[cut:, c : c + chunk] = totals[1][at + cut - half : at + rows - half]
            at += rows


def finish(firsts, seconds, pair_shape, lower_shape):
    half, chunk = firsts[0].shape[-2:]

    def leading(array):
        lead = array.ndim - 2
        return pl.BlockSpec((None,) * lead + (half, chunk), lambda i, n=lead: (0,) * (n + 2))

    return pl.pallas_call(
        functools.partial(finish_kernel, len(firsts), chunk),
        grid=(1,),
        in_specs=[leading(a) for a in firsts + seconds],
        out_specs=[
            pl.BlockSpec(pair_shape, lambda i: (0, 0)),
            pl.BlockSpec(lower_shape, lambda i: (0, 0)),
        ],
        out_shape=[
            jax.ShapeDtypeStruct(pair_shape, F32),
            jax.ShapeDtypeStruct(lower_shape, F32),
        ],
        compiler_params=params(1, 24),
        name="finish",
    )(*firsts, *seconds)


def local(tokens_in, out_grad, expert_ids, gate_weights, w_gate_up, w_down):
    tok_rows, width = tokens_in.shape
    top = expert_ids.shape[1]
    group = lax.axis_size("expert")
    replicas = lax.axis_size("dp")
    units = w_down.shape[1]
    capacity = 5 * tok_rows * top // (4 * group)
    chunk = math.gcd(units, width)
    me = lax.axis_index("expert").astype(jnp.int32)
    replica = lax.axis_index("dp").astype(jnp.int32)
    place = me.reshape(1)
    meta = jnp.concatenate([expert_ids.astype(F32), gate_weights], axis=1).T
    w_pair, w_lower = w_gate_up[0], w_down[0]

    def move(array, pairs):
        return lax.ppermute(array, "expert", pairs)

    def swap(array, m):
        return move(array, [(i, i ^ m) for i in range(group)])

    def after(array, *others):
        return lax.optimization_barrier((array, *others))[0]

    if group == 4 and tok_rows < 2 * capacity:
        far = [(0, 2), (3, 1)]
        far_meta, far_rows, far_grads = move(meta, far), move(tokens_in, far), move(out_grad, far)
        x0, g0, pair1, x2, g2, x3, g3 = pack(
            place, meta, tokens_in, out_grad, [0, 1, 2, 3], [1], capacity
        )
        pair1 = swap(after(pair1, far_rows), 1)
        cx, cg, onward = pack(place, far_meta, far_rows, far_grads, [0, 1], [1], capacity)
        onward = move(onward, [(2, 3), (1, 0)])
        x3 = move(x3, [(1, 2), (2, 1)])
        x2 = move(x2, [(1, 3), (2, 0)])
        g3 = move(after(g3, x3), [(1, 2), (2, 1)])
        g2 = move(after(g2, x2), [(1, 3), (2, 0)])
        inputs = [[x0], [pair1], [cx, x2], [onward, x3]]
        grads = [[g0], [pair1], [cg, g2], [onward, g3]]
    else:
        offsets = list(range(group))
        packed = pack(place, meta, tokens_in, out_grad, offsets, [], capacity)
        moved = [packed[2 * m : 2 * m + 2] for m in offsets]
        moved = [moved[0]] + [[swap(a, m) for a in moved[m]] for m in offsets[1:]]
        inputs, grads = [[a] for a, _ in moved], [[b] for _, b in moved]

    lead = group // 2
    early_d = forward(0, inputs[:lead], w_pair, [])
    late_d = forward(1, inputs[lead:], w_pair, early_d[2:])
    early = inner(0, grads[:lead], w_lower, *early_d[:2], w_pair, [])
    late = inner(1, grads[lead:], w_lower, *late_d[:2], w_pair, early[lead:])
    blocks = list(early[:lead]) + list(late[:lead])
    returned = [blocks[0]] + [swap(blocks[m], m) for m in range(1, group)]

    shares = replicas // 2
    own = [replica ^ (2 * r) for r in range(shares)]
    operands = (late_d[3], late_d[2], *late[lead:])
    given = give(jnp.stack(own) ^ 1, *operands, replicas, chunk)
    came = lax.ppermute(given, "dp", [(i, i ^ 1) for i in range(replicas)])
    mine = give(after(jnp.stack(own), given), *operands, replicas, chunk)
    bits = list(range(shares.bit_length() - 1))
    middle = len(bits) // 2
    first_bits, second_bits = bits, bits[middle:] + bits[:middle]
    kept_a, sent_a, kept_b, sent_b = split(mine, came, first_bits[0], second_bits[0])
    firsts = halvings(kept_a, sent_a, first_bits)
    seconds = halvings(kept_b, sent_b, second_bits)
    *returned, firsts[1], seconds[1] = lax.optimization_barrier((*returned, firsts[1], seconds[1]))
    grad_tokens = combine(place, meta, returned)
    pair_sum, lower_sum = finish(
        firsts, seconds, (width // replicas, 2 * units), (units // replicas, width)
    )
    return (grad_tokens, pair_sum, lower_sum)


def solution(mesh):
    in_specs = (
        P(("dp", "expert"), None),
        P(("dp", "expert"), None),
        P(("dp", "expert"), None),
        P(("dp", "expert"), None),
        P("expert", None, None),
        P("expert", None, None),
    )
    out_specs = (P(("dp", "expert"), None), P("dp", "expert"), P("dp", "expert"))
    return jax.shard_map(local, mesh=mesh, in_specs=in_specs, out_specs=out_specs, check_vma=False)
```

```python
import functools
import math

import jax
import jax.numpy as jnp
from jax import lax
from jax.experimental import pallas as pl
from jax.experimental.pallas import tpu as pltpu
from jax.sharding import PartitionSpec as P

F32 = jnp.float32
BF16 = jnp.bfloat16
MIB = 1024 * 1024


def params(grid_rank, mebibytes):
    return pltpu.CompilerParams(
        dimension_semantics=("arbitrary",) * grid_rank, vmem_limit_bytes=mebibytes * MIB
    )


def cost(macs):
    return pl.CostEstimate(flops=2 * macs, bytes_accessed=1, transcendentals=0)


FREE = pl.CostEstimate(flops=1, bytes_accessed=1, transcendentals=0)


def whole(array):
    rank = array.ndim
    return pl.BlockSpec(
        array.shape, lambda *at: (0,) * rank, pipeline_mode=pl.Buffered(buffer_count=1)
    )


def dot(a, b):
    return lax.dot_general(a, b, (((1,), (0,)), ((), ())), preferred_element_type=F32)


def dot_nt(a, b):
    return lax.dot_general(a, b, (((1,), (1,)), ((), ())), preferred_element_type=F32)


def pick_matrices(me, ids, offsets, capacity):
    top, rows = ids.shape
    lines = max(8, max(offsets) + 1)
    wanted = (lax.broadcasted_iota(jnp.int32, (lines, rows), 0) ^ me).astype(F32)
    named = ids[0:1, :] == wanted
    for k in range(1, top):
        named = named | (ids[k : k + 1, :] == wanted)
    named = named.astype(F32)
    before = lax.broadcasted_iota(jnp.int32, (rows, rows), 0) <= lax.broadcasted_iota(
        jnp.int32, (rows, rows), 1
    )
    place = dot(named.astype(BF16), before.astype(F32).astype(BF16))
    place = jnp.where(named > 0, place - 1.0, -1.0)
    slots = lax.broadcasted_iota(jnp.int32, (capacity, rows), 0).astype(F32)
    return [(place[m : m + 1, :] == slots).astype(F32) for m in offsets]


def pieces_of(ids, gates):
    lines, rest = [ids.T.astype(BF16)], gates.T
    for _ in range(3):
        term = lax.reduce_precision(rest, 8, 7)
        lines.append(term.astype(BF16))
        rest = rest - term
    lines = jnp.concatenate(lines, axis=0)
    return jnp.pad(lines, ((0, -lines.shape[0] % 16), (0, 0)))


def ids_and_gates(meta, top):
    meta = meta.astype(F32)
    terms = [meta[top * (1 + i) : top * (2 + i)] for i in range(3)]
    return meta[:top], (terms[2] + terms[1]) + terms[0]


def pack_kernel(offsets, joint, top, kinds, me_ref, meta_ref, *rest):
    sources, outs, (pick, gain) = rest[: len(kinds)], list(rest[len(kinds) : -2]), rest[-2:]
    capacity = pick.shape[1]

    @pl.when(pl.program_id(0) == 0)
    def _():
        me = me_ref[0]
        ids, gates = ids_and_gates(meta_ref[...], top)
        for at, matrix in enumerate(pick_matrices(me, ids, offsets, capacity)):
            pick[at] = matrix.astype(BF16)
            chosen = jnp.where(ids == (me ^ offsets[at]).astype(F32), gates, 0.0)
            weight = jnp.sum(chosen, axis=0, keepdims=True)
            gain[at] = jnp.broadcast_to(
                jnp.sum(matrix * weight, axis=1, keepdims=True), gain.shape[1:]
            )

    for at, m in enumerate(offsets):
        out = outs.pop(0) if m in joint else None
        for which, (kind, source) in enumerate(zip(kinds, sources, strict=True)):
            rows = dot(pick[at], source[...])
            if kind == "grads":
                rows = rows * gain[at][:, 0:1]
            if out is None:
                outs.pop(0)[...] = rows.astype(BF16)
            else:
                out[which] = rows.astype(BF16)


def pack(me, meta, sources, offsets, joint, capacity, top):
    rows, width = next(iter(sources.values())).shape
    block = min(width, 512)
    count = len(offsets)
    out_specs, out_shape = [], []
    for m in offsets:
        if m in joint:
            lead = len(sources)
            out_specs.append(pl.BlockSpec((lead, capacity, block), lambda i: (0, 0, i)))
            out_shape.append(jax.ShapeDtypeStruct((lead, capacity, width), BF16))
        else:
            out_specs += [pl.BlockSpec((capacity, block), lambda i: (0, i))] * len(sources)
            out_shape += [jax.ShapeDtypeStruct((capacity, width), BF16)] * len(sources)
    return pl.pallas_call(
        functools.partial(pack_kernel, offsets, joint, top, list(sources)),
        grid=(width // block,),
        in_specs=[
            pl.BlockSpec(memory_space=pltpu.SMEM),
            pl.BlockSpec(meta.shape, lambda i: (0, 0)),
        ]
        + [pl.BlockSpec((rows, block), lambda i: (0, i))] * len(sources),
        out_specs=out_specs,
        out_shape=out_shape,
        scratch_shapes=[
            pltpu.VMEM((count, capacity, rows), BF16),
            pltpu.VMEM((count, capacity, 128), F32),
        ],
        compiler_params=params(1, 14),
        cost_estimate=FREE,
        name="pack",
    )(me, meta, *sources.values())


def combine_kernel(group, top, me_ref, meta_ref, *refs):
    blocks, out, pick = refs[:group], refs[group], refs[group + 1]
    capacity = blocks[0].shape[0]

    @pl.when(pl.program_id(0) == 0)
    def _():
        ids, _ = ids_and_gates(meta_ref[...], top)
        matrices = pick_matrices(me_ref[0], ids, list(range(group)), capacity)
        for m, matrix in enumerate(matrices):
            pick[m] = matrix.T.astype(BF16)

    total = dot(pick[0], blocks[0][...])
    for m in range(1, group):
        total += dot(pick[m], blocks[m][...])
    out[...] = total.astype(BF16)


def combine(me, meta, blocks, top):
    group, (capacity, width) = len(blocks), blocks[0].shape
    rows = meta.shape[1]
    block = min(width, 512)
    return pl.pallas_call(
        functools.partial(combine_kernel, group, top),
        grid=(width // block,),
        in_specs=[
            pl.BlockSpec(memory_space=pltpu.SMEM),
            pl.BlockSpec(meta.shape, lambda i: (0, 0)),
        ]
        + [pl.BlockSpec((capacity, block), lambda i: (0, i))] * group,
        out_specs=pl.BlockSpec((rows, block), lambda i: (0, i)),
        out_shape=jax.ShapeDtypeStruct((rows, width), BF16),
        scratch_shapes=[pltpu.VMEM((group, rows, capacity), BF16)],
        compiler_params=params(1, 10),
        cost_estimate=FREE,
        name="combine",
    )(me, meta, *blocks)


def parts_of(capacity, group):
    own = -(-capacity // 128) * 128
    others = -(-(group - 1) * capacity // own) * own
    return own + others, {True: (own, others // own), False: (others, 0)}


def gather_rows(parts, sizes, held):
    at, parts = 0, list(parts)
    for size in sizes:
        mine, parts = parts[:size], parts[size:]
        rows = mine[0][...]
        for other in mine[1:]:
            rows = rows + other[...]
        held[at : at + rows.shape[0], :] = rows
        at += rows.shape[0]
    if at < held.shape[0]:
        held[at:, :] = jnp.zeros((held.shape[0] - at, held.shape[1]), held.dtype)


def part_spec(array, capacity):
    block = (capacity, array.shape[1])
    return pl.BlockSpec(block, lambda i: (0, 0), pipeline_mode=pl.Buffered(buffer_count=1))


def forward_kernel(sizes, *refs):
    count = sum(sizes)
    gate_w, up_w = refs[count : count + 2]
    gate_out, up_out, hidden_out, flipped, held = refs[-5:]

    @pl.when(pl.program_id(0) == 0)
    def _():
        gather_rows(refs[:count], sizes, held)
        step = min(held.shape[1], 256)
        for d in range(0, held.shape[1], step):
            flipped[d : d + step, :] = held[:, d : d + step].T

    gate, up = dot(held[...], gate_w[...]), dot(held[...], up_w[...])
    sigmoid = jax.nn.sigmoid(gate)
    swish = gate * sigmoid
    gate_out[...] = (up * sigmoid * (1.0 + gate * (1.0 - sigmoid))).astype(BF16)
    up_out[...] = swish.astype(BF16)
    hidden_out[...] = (swish * up).T.astype(BF16)


def forward(group, sources, w_pair, before):
    arrays, sizes = sum(sources, []), [len(s) for s in sources]
    capacity, width = min(a.shape[0] for a in arrays), arrays[0].shape[1]
    units = w_pair.shape[1] // 2
    tile = math.gcd(units, 256)
    tiles = units // tile
    total, parts = parts_of(capacity, group)
    rows, part = parts[not before]
    shapes = [
        jax.ShapeDtypeStruct((rows, units), BF16),
        jax.ShapeDtypeStruct((rows, units), BF16),
        jax.ShapeDtypeStruct((units, total), BF16),
        jax.ShapeDtypeStruct((width, total), BF16),
    ]
    first = len(arrays) + 2
    return pl.pallas_call(
        functools.partial(forward_kernel, sizes),
        grid=(tiles,),
        in_specs=[part_spec(a, capacity) for a in arrays]
        + [
            pl.BlockSpec((width, tile), lambda j: (0, j)),
            pl.BlockSpec((width, tile), lambda j: (0, tiles + j)),
        ]
        + [pl.BlockSpec(memory_space=pl.ANY) for _ in before],
        out_specs=[
            pl.BlockSpec((rows, tile), lambda j: (0, j)),
            pl.BlockSpec((rows, tile), lambda j: (0, j)),
            pl.BlockSpec((tile, rows), lambda j: (j, part)),
            pl.BlockSpec((width, rows), lambda j: (0, part)),
        ],
        out_shape=shapes,
        scratch_shapes=[pltpu.VMEM((rows, width), BF16)],
        input_output_aliases={first + i: 2 + i for i in range(len(before))},
        compiler_params=params(1, 20),
        cost_estimate=cost(rows * width * units),
        name="forward",
    )(*arrays, w_pair, w_pair, *before)


def inner_kernel(sizes, tiles, rows, *refs):
    count, sources = sum(sizes), len(sizes)
    down_w, gate_d, up_d, w_ref = refs[count : count + 4]
    outs, (grads, gate_out, up_out, grad_pre) = refs[-4 - sources : -4], refs[-4:]
    step = pl.program_id(0)
    units = grad_pre.shape[1] // 2

    @pl.when(step == 0)
    def _():
        gather_rows(refs[:count], sizes, grads)

    for j in range(tiles):

        @pl.when(step == j)
        def _():
            grad_hidden = dot_nt(grads[:rows, :], down_w[...])
            tile = grad_hidden.shape[1]
            for at, slope, out in ((0, gate_d, gate_out), (units, up_d, up_out)):
                value = (grad_hidden * slope[:rows, :].astype(F32)).astype(BF16)
                grad_pre[:, at + j * tile : at + (j + 1) * tile] = value
                out[:rows, :] = value
                if rows < out.shape[0]:
                    out[rows:, :] = jnp.zeros((out.shape[0] - rows, tile), BF16)

    @pl.when(step >= tiles)
    def _():
        back = dot_nt(grad_pre[...], w_ref[...])
        capacity = rows // sources
        for m, out in enumerate(outs):
            out[...] = back[m * capacity : (m + 1) * capacity, :].astype(BF16)


def inner(group, sources, w_down, gate_d, up_d, w_pair, before):
    arrays, sizes = sum(sources, []), [len(s) for s in sources]
    capacity, width = min(a.shape[0] for a in arrays), arrays[0].shape[1]
    units = w_down.shape[0]
    tile = math.gcd(units, 256)
    tiles = units // tile
    block = min(width, 512)
    rows = len(sources) * capacity
    total, parts = parts_of(capacity, group)
    held, part = parts[not before]

    def tile_at(i):
        return jnp.minimum(i, tiles - 1)

    def block_at(i):
        return jnp.maximum(i - tiles, 0)

    first, outs = len(arrays) + 4, len(sources)
    return pl.pallas_call(
        functools.partial(inner_kernel, sizes, tiles, rows),
        grid=(tiles + width // block,),
        in_specs=[part_spec(a, capacity) for a in arrays]
        + [
            pl.BlockSpec((tile, width), lambda i: (tile_at(i), 0)),
            pl.BlockSpec((held, tile), lambda i: (0, tile_at(i))),
            pl.BlockSpec((held, tile), lambda i: (0, tile_at(i))),
            pl.BlockSpec((block, 2 * units), lambda i: (block_at(i), 0)),
        ]
        + [pl.BlockSpec(memory_space=pl.ANY) for _ in before],
        out_specs=[pl.BlockSpec((capacity, block), lambda i: (0, block_at(i)))] * outs
        + [
            pl.BlockSpec((held, width), lambda i: (part, 0)),
            pl.BlockSpec((held, tile), lambda i: (part, tile_at(i))),
            pl.BlockSpec((held, tile), lambda i: (part, tile_at(i))),
        ],
        out_shape=[jax.ShapeDtypeStruct((capacity, width), BF16)] * outs
        + [
            jax.ShapeDtypeStruct((total, width), BF16),
            jax.ShapeDtypeStruct((total, units), BF16),
            jax.ShapeDtypeStruct((total, units), BF16),
        ],
        scratch_shapes=[pltpu.VMEM((rows, 2 * units), BF16)],
        input_output_aliases={first + i: outs + i for i in range(len(before))},
        compiler_params=params(1, 20),
        cost_estimate=FREE,
        name="inner",
    )(*arrays, w_down, gate_d, up_d, w_pair, *before)


def pair_chunks(flipped_rows, sides, chunk):
    for side in sides:
        for c in range(0, side.shape[1], chunk):
            yield dot(flipped_rows, side[:, c : c + chunk])


def lower_share(rows, chunk):
    return jnp.concatenate([rows[:, c : c + chunk] for c in range(0, rows.shape[1], chunk)], axis=0)


def hold_lower(which, shares, hidden_ref, rows, lower):
    own = hidden_ref.shape[1]
    stacked = jnp.concatenate(
        [hidden_ref[which(r)].astype(F32) for r in range(shares)], axis=0
    ).astype(BF16)
    lower[...] = dot(stacked, rows).reshape(shares, own, rows.shape[1])


def give_kernel(shares, chunk, which_ref, flip_ref, hidden_ref, grads, gate, up, out, lower):
    step = pl.program_id(0)

    @pl.when(step == 0)
    def _():
        hold_lower(lambda r: which_ref[r], shares, hidden_ref, grads[...], lower)

    at = 0
    for piece in pair_chunks(flip_ref[0], (gate[...], up[...]), chunk):
        out[0, at : at + piece.shape[0]] = piece.astype(BF16)
        at += piece.shape[0]
    out[0, at:] = lower_share(lower[step], chunk).astype(BF16)


def shared_operands(flipped, hidden, replicas):
    width, rows = flipped.shape
    units = hidden.shape[0]
    return (
        flipped.reshape(replicas, width // replicas, rows),
        hidden.reshape(replicas, units // replicas, rows),
    )


def give(which, flipped, hidden, grads, gate, up, replicas, chunk):
    rows, width = grads.shape
    units = gate.shape[1]
    shares = replicas // 2
    share_rows = (2 * units * (width // replicas) + (units // replicas) * width) // chunk
    flipped, hidden = shared_operands(flipped, hidden, replicas)
    return pl.pallas_call(
        functools.partial(give_kernel, shares, chunk),
        grid_spec=pltpu.PrefetchScalarGridSpec(
            num_scalar_prefetch=1,
            grid=(shares,),
            in_specs=[pl.BlockSpec((1, width // replicas, rows), lambda i, w: (w[i], 0, 0))]
            + [whole(a) for a in (hidden, grads, gate, up)],
            out_specs=pl.BlockSpec((1, share_rows, chunk), lambda i, w: (i, 0, 0)),
            scratch_shapes=[pltpu.VMEM((shares, units // replicas, width), F32)],
        ),
        out_shape=jax.ShapeDtypeStruct((shares, share_rows, chunk), BF16),
        compiler_params=params(1, 18),
        cost_estimate=FREE,
        name="give",
    )(which, flipped, hidden, grads, gate, up)


def split_kernel(shares, own, came, *outs):
    step = pl.program_id(0)
    total = own[0].astype(F32) + came[0].astype(F32)
    half = total.shape[0] // 2
    for r in range(shares):

        @pl.when(step == r)
        def _():
            outs[2 * r][...] = total[:half].astype(BF16)
            outs[2 * r + 1][...] = total[half:].astype(BF16)


def split(own, came):
    shares, share_rows, chunk = came.shape
    half = share_rows // 2
    share = pl.BlockSpec((1, share_rows, chunk), lambda i: (i, 0, 0))
    halves = pl.pallas_call(
        functools.partial(split_kernel, shares),
        grid=(shares,),
        in_specs=[share, share],
        out_specs=[pl.BlockSpec((half, chunk), lambda i: (0, 0))] * (2 * shares),
        out_shape=[jax.ShapeDtypeStruct((half, chunk), BF16)] * (2 * shares),
        compiler_params=params(1, 18),
        cost_estimate=FREE,
        name="split",
    )(own, came)
    return halves[::2], halves[1::2]


def halvings(shares, bits, before_last):
    terms = {r: [share] for r, share in enumerate(shares)}
    for bit in bits:
        pairs = [(i, i ^ (2 << bit)) for i in range(lax.axis_size("dp"))]
        for r in sorted((r for r in terms if (r >> bit) & 1), reverse=True):
            mine = terms.pop(r)
            if len(mine) > 1:
                mine = [sum(term.astype(F32) for term in mine).astype(BF16)]
            if bit == bits[-1]:
                mine = lax.optimization_barrier((mine[0], before_last))
            terms[r ^ (1 << bit)].append(lax.ppermute(mine[0], "dp", pairs))
    return terms[0]


def finish_kernel(count, chunk, *refs):
    halves, (pair, lower) = (refs[:count], refs[count : 2 * count]), refs[2 * count :]
    totals = []
    for terms in halves:
        total = terms[0][...].astype(F32)
        for term in terms[1:]:
            total += term[...].astype(F32)
        totals.append(total)
    half = totals[0].shape[0]
    at = 0
    for out in (pair, lower):
        rows, columns = out.shape
        for c in range(0, columns, chunk):
            cut = min(max(half - at, 0), rows)
            if cut:
                out[:cut, c : c + chunk] = totals[0][at : at + cut]
            if cut < rows:
                out[cut:, c : c + chunk] = totals[1][at + cut - half : at + rows - half]
            at += rows


def finish(firsts, seconds, pair_shape, lower_shape):
    chunk = firsts[0].shape[1]
    return pl.pallas_call(
        functools.partial(finish_kernel, len(firsts), chunk),
        grid=(1,),
        in_specs=[pl.BlockSpec(a.shape, lambda i: (0, 0)) for a in firsts + seconds],
        out_specs=[
            pl.BlockSpec(pair_shape, lambda i: (0, 0)),
            pl.BlockSpec(lower_shape, lambda i: (0, 0)),
        ],
        out_shape=[
            jax.ShapeDtypeStruct(pair_shape, F32),
            jax.ShapeDtypeStruct(lower_shape, F32),
        ],
        compiler_params=params(1, 24),
        cost_estimate=FREE,
        name="finish",
    )(*firsts, *seconds)


def local(tokens_in, out_grad, expert_ids, gate_weights, w_gate_up, w_down):
    tok_rows, width = tokens_in.shape
    top = expert_ids.shape[1]
    group = lax.axis_size("expert")
    replicas = lax.axis_size("dp")
    units = w_down.shape[1]
    capacity = 5 * tok_rows * top // (4 * group)
    chunk = math.gcd(units, width)
    me = lax.axis_index("expert").astype(jnp.int32)
    replica = lax.axis_index("dp").astype(jnp.int32)
    place = me.reshape(1)
    meta = pieces_of(expert_ids, gate_weights)
    w_pair, w_lower = w_gate_up[0], w_down[0]

    def move(array, pairs):
        return lax.ppermute(array, "expert", pairs)

    def swap(array, m):
        return move(array, [(i, i ^ m) for i in range(group)])

    def after(array, *others):
        return lax.optimization_barrier((array, *others))[0]

    if group == 4 and tok_rows < 2 * capacity:
        far, near, cross = [(0, 2), (3, 1)], [(1, 2), (2, 1)], [(1, 3), (2, 0)]
        far_meta = move(meta, far)
        far_rows = move(after(tokens_in, far_meta), far)
        x0, g0, x1, g1, x2, g2, x3, g3 = pack(
            place, meta, dict(tokens=tokens_in, grads=out_grad), [0, 1, 2, 3], [], capacity, top
        )
        x1, x3, x2 = swap(x1, 1), move(x3, near), move(x2, cross)
        cx, onward = pack(place, far_meta, dict(tokens=far_rows), [0, 1], [], capacity + 16, top)
        onward = move(onward, [(2, 3), (1, 0)])
        g1 = swap(after(g1, x1), 1)
        g2 = swap(after(g2, x3), 2)
        g3 = swap(after(g3, x2), 3)
        inputs, grads = [[x0], [x1], [cx, x2], [onward, x3]], [[g0], [g1], [g2], [g3]]
    else:
        offsets = list(range(group))
        packed = pack(
            place, meta, dict(tokens=tokens_in, grads=out_grad), offsets, [], capacity, top
        )
        moved = [packed[2 * m : 2 * m + 2] for m in offsets]
        moved = [moved[0]] + [[swap(a, m) for a in moved[m]] for m in offsets[1:]]
        inputs, grads = [[a] for a, _ in moved], [[b] for _, b in moved]

    own_d = forward(group, inputs[:1], w_pair, [])
    others_d = forward(group, inputs[1:], w_pair, own_d[2:])
    own_back, *own_grads = inner(group, grads[:1], w_lower, *own_d[:2], w_pair, [])
    late = inner(group, grads[1:], w_lower, *others_d[:2], w_pair, own_grads)
    returned = [own_back, *late[: group - 1]]
    for m in range(group - 1, 0, -1):
        ahead = returned[m + 1 :] if 2 * m >= group else []
        returned[m] = swap(after(returned[m], *ahead), m)

    shares = replicas // 2
    own = [replica ^ (2 * r) for r in range(shares)]
    operands = (others_d[3], others_d[2], *late[group - 1 :])
    first_own = jnp.stack(own) ^ 1
    given = give(first_own, *operands, replicas, chunk)
    came = lax.ppermute(given, "dp", [(i, i ^ 1) for i in range(replicas)])
    mine = give(after(jnp.stack(own), given), *operands, replicas, chunk)
    bits = list(range(shares.bit_length() - 1))
    middle = len(bits) // 2
    first_bits, second_bits = bits, bits[middle:] + bits[:middle]
    first, second = split(mine, came)
    firsts = halvings(first, first_bits, returned[-1])
    seconds = halvings(second, second_bits, returned[-1])
    pair_sum, lower_sum = finish(
        firsts, seconds, (width // replicas, 2 * units), (units // replicas, width)
    )
    *returned, pair_sum, lower_sum = lax.optimization_barrier((*returned, pair_sum, lower_sum))
    grad_tokens = combine(place, meta, returned, top)
    return (grad_tokens, pair_sum, lower_sum)


def solution(mesh):
    in_specs = (
        P(("dp", "expert"), None),
        P(("dp", "expert"), None),
        P(("dp", "expert"), None),
        P(("dp", "expert"), None),
        P("expert", None, None),
        P("expert", None, None),
    )
    out_specs = (P(("dp", "expert"), None), P("dp", "expert"), P("dp", "expert"))
    return jax.shard_map(local, mesh=mesh, in_specs=in_specs, out_specs=out_specs, check_vma=False)
```

```python
import functools
import math

import jax
import jax.numpy as jnp
from jax import lax
from jax.experimental import pallas as pl
from jax.experimental.pallas import tpu as pltpu
from jax.sharding import PartitionSpec as P

F32 = jnp.float32
BF16 = jnp.bfloat16
MIB = 1024 * 1024


def params(grid_rank, mebibytes):
    return pltpu.CompilerParams(
        dimension_semantics=("arbitrary",) * grid_rank, vmem_limit_bytes=mebibytes * MIB
    )


def cost(macs):
    return pl.CostEstimate(flops=2 * macs, bytes_accessed=1, transcendentals=0)


FREE = pl.CostEstimate(flops=1, bytes_accessed=1, transcendentals=0)


def whole(array):
    rank = array.ndim
    return pl.BlockSpec(
        array.shape, lambda *at: (0,) * rank, pipeline_mode=pl.Buffered(buffer_count=1)
    )


def dot(a, b):
    return lax.dot_general(a, b, (((1,), (0,)), ((), ())), preferred_element_type=F32)


def dot_nt(a, b):
    return lax.dot_general(a, b, (((1,), (1,)), ((), ())), preferred_element_type=F32)


def pick_matrices(me, ids, offsets, capacity):
    top, rows = ids.shape
    lines = max(8, max(offsets) + 1)
    wanted = (lax.broadcasted_iota(jnp.int32, (lines, rows), 0) ^ me).astype(F32)
    named = ids[0:1, :] == wanted
    for k in range(1, top):
        named = named | (ids[k : k + 1, :] == wanted)
    named = named.astype(F32)
    before = lax.broadcasted_iota(jnp.int32, (rows, rows), 0) <= lax.broadcasted_iota(
        jnp.int32, (rows, rows), 1
    )
    place = dot(named.astype(BF16), before.astype(F32).astype(BF16))
    place = jnp.where(named > 0, place - 1.0, -1.0)
    slots = lax.broadcasted_iota(jnp.int32, (capacity, rows), 0).astype(F32)
    return [(place[m : m + 1, :] == slots).astype(F32) for m in offsets]


def pieces_of(ids, gates):
    lines, rest = [ids.T.astype(BF16)], gates.T
    for _ in range(3):
        term = lax.reduce_precision(rest, 8, 7)
        lines.append(term.astype(BF16))
        rest = rest - term
    lines = jnp.concatenate(lines, axis=0)
    return jnp.pad(lines, ((0, -lines.shape[0] % 16), (0, 0)))


def ids_and_gates(meta, top):
    meta = meta.astype(F32)
    terms = [meta[top * (1 + i) : top * (2 + i)] for i in range(3)]
    return meta[:top], (terms[2] + terms[1]) + terms[0]


def pack_kernel(offsets, joint, top, kinds, me_ref, meta_ref, *rest):
    sources, outs, (pick, gain) = rest[: len(kinds)], list(rest[len(kinds) : -2]), rest[-2:]
    capacity = pick.shape[1]

    @pl.when(pl.program_id(0) == 0)
    def _():
        me = me_ref[0]
        ids, gates = ids_and_gates(meta_ref[...], top)
        for at, matrix in enumerate(pick_matrices(me, ids, offsets, capacity)):
            pick[at] = matrix.astype(BF16)
            chosen = jnp.where(ids == (me ^ offsets[at]).astype(F32), gates, 0.0)
            weight = jnp.sum(chosen, axis=0, keepdims=True)
            gain[at] = jnp.broadcast_to(
                jnp.sum(matrix * weight, axis=1, keepdims=True), gain.shape[1:]
            )

    for at, m in enumerate(offsets):
        out = outs.pop(0) if m in joint else None
        for which, (kind, source) in enumerate(zip(kinds, sources, strict=True)):
            rows = dot(pick[at], source[...])
            if kind == "grads":
                rows = rows * gain[at][:, 0:1]
            if out is None:
                outs.pop(0)[...] = rows.astype(BF16)
            else:
                out[which] = rows.astype(BF16)


def pack(me, meta, sources, offsets, joint, capacity, top):
    rows, width = next(iter(sources.values())).shape
    block = min(width, 512)
    count = len(offsets)
    out_specs, out_shape = [], []
    for m in offsets:
        if m in joint:
            lead = len(sources)
            out_specs.append(pl.BlockSpec((lead, capacity, block), lambda i: (0, 0, i)))
            out_shape.append(jax.ShapeDtypeStruct((lead, capacity, width), BF16))
        else:
            out_specs += [pl.BlockSpec((capacity, block), lambda i: (0, i))] * len(sources)
            out_shape += [jax.ShapeDtypeStruct((capacity, width), BF16)] * len(sources)
    return pl.pallas_call(
        functools.partial(pack_kernel, offsets, joint, top, list(sources)),
        grid=(width // block,),
        in_specs=[
            pl.BlockSpec(memory_space=pltpu.SMEM),
            pl.BlockSpec(meta.shape, lambda i: (0, 0)),
        ]
        + [pl.BlockSpec((rows, block), lambda i: (0, i))] * len(sources),
        out_specs=out_specs,
        out_shape=out_shape,
        scratch_shapes=[
            pltpu.VMEM((count, capacity, rows), BF16),
            pltpu.VMEM((count, capacity, 128), F32),
        ],
        compiler_params=params(1, 14),
        cost_estimate=FREE,
        name="pack",
    )(me, meta, *sources.values())


def combine_kernel(group, top, me_ref, meta_ref, *refs):
    blocks, out, pick = refs[:group], refs[group], refs[group + 1]
    capacity = blocks[0].shape[0]

    @pl.when(pl.program_id(0) == 0)
    def _():
        ids, _ = ids_and_gates(meta_ref[...], top)
        matrices = pick_matrices(me_ref[0], ids, list(range(group)), capacity)
        for m, matrix in enumerate(matrices):
            pick[m] = matrix.T.astype(BF16)

    total = dot(pick[0], blocks[0][...])
    for m in range(1, group):
        total += dot(pick[m], blocks[m][...])
    out[...] = total.astype(BF16)


def combine(me, meta, blocks, top):
    group, (capacity, width) = len(blocks), blocks[0].shape
    rows = meta.shape[1]
    block = min(width, 512)
    return pl.pallas_call(
        functools.partial(combine_kernel, group, top),
        grid=(width // block,),
        in_specs=[
            pl.BlockSpec(memory_space=pltpu.SMEM),
            pl.BlockSpec(meta.shape, lambda i: (0, 0)),
        ]
        + [pl.BlockSpec((capacity, block), lambda i: (0, i))] * group,
        out_specs=pl.BlockSpec((rows, block), lambda i: (0, i)),
        out_shape=jax.ShapeDtypeStruct((rows, width), BF16),
        scratch_shapes=[pltpu.VMEM((group, rows, capacity), BF16)],
        compiler_params=params(1, 10),
        cost_estimate=FREE,
        name="combine",
    )(me, meta, *blocks)


def parts_of(capacity, group):
    own = -(-capacity // 128) * 128
    others = -(-(group - 1) * capacity // own) * own
    return own + others, {True: (own, others // own), False: (others, 0)}


def gather_rows(parts, sizes, held):
    at, parts = 0, list(parts)
    for size in sizes:
        mine, parts = parts[:size], parts[size:]
        rows = mine[0][...]
        for other in mine[1:]:
            rows = rows + other[...]
        held[at : at + rows.shape[0], :] = rows
        at += rows.shape[0]
    if at < held.shape[0]:
        held[at:, :] = jnp.zeros((held.shape[0] - at, held.shape[1]), held.dtype)


def part_spec(array, capacity):
    block = (capacity, array.shape[1])
    return pl.BlockSpec(block, lambda i: (0, 0), pipeline_mode=pl.Buffered(buffer_count=1))


def forward_kernel(sizes, *refs):
    count = sum(sizes)
    gate_w, up_w = refs[count : count + 2]
    gate_out, up_out, hidden_out, flipped, held = refs[-5:]

    @pl.when(pl.program_id(0) == 0)
    def _():
        gather_rows(refs[:count], sizes, held)
        step = min(held.shape[1], 256)
        for d in range(0, held.shape[1], step):
            flipped[d : d + step, :] = held[:, d : d + step].T

    gate, up = dot(held[...], gate_w[...]), dot(held[...], up_w[...])
    sigmoid = jax.nn.sigmoid(gate)
    swish = gate * sigmoid
    gate_out[...] = (up * sigmoid * (1.0 + gate * (1.0 - sigmoid))).astype(BF16)
    up_out[...] = swish.astype(BF16)
    hidden_out[...] = (swish * up).T.astype(BF16)


def forward(group, sources, w_pair, before):
    arrays, sizes = sum(sources, []), [len(s) for s in sources]
    capacity, width = min(a.shape[0] for a in arrays), arrays[0].shape[1]
    units = w_pair.shape[1] // 2
    tile = math.gcd(units, 256)
    tiles = units // tile
    total, parts = parts_of(capacity, group)
    rows, part = parts[not before]
    shapes = [
        jax.ShapeDtypeStruct((rows, units), BF16),
        jax.ShapeDtypeStruct((rows, units), BF16),
        jax.ShapeDtypeStruct((units, total), BF16),
        jax.ShapeDtypeStruct((width, total), BF16),
    ]
    first = len(arrays) + 2
    return pl.pallas_call(
        functools.partial(forward_kernel, sizes),
        grid=(tiles,),
        in_specs=[part_spec(a, capacity) for a in arrays]
        + [
            pl.BlockSpec((width, tile), lambda j: (0, j)),
            pl.BlockSpec((width, tile), lambda j: (0, tiles + j)),
        ]
        + [pl.BlockSpec(memory_space=pl.ANY) for _ in before],
        out_specs=[
            pl.BlockSpec((rows, tile), lambda j: (0, j)),
            pl.BlockSpec((rows, tile), lambda j: (0, j)),
            pl.BlockSpec((tile, rows), lambda j: (j, part)),
            pl.BlockSpec((width, rows), lambda j: (0, part)),
        ],
        out_shape=shapes,
        scratch_shapes=[pltpu.VMEM((rows, width), BF16)],
        input_output_aliases={first + i: 2 + i for i in range(len(before))},
        compiler_params=params(1, 20),
        cost_estimate=cost(rows * width * units),
        name="forward",
    )(*arrays, w_pair, w_pair, *before)


def inner_kernel(sizes, rows, tiles, *refs):
    count = sum(sizes)
    down_w, gate_d, up_d, w_ref = refs[count : count + 4]
    last, grads, gate_out, up_out, grad_pre = refs[-5:]
    step = pl.program_id(0)
    units, capacity = grad_pre.shape[1] // 2, last.shape[0]

    @pl.when(step == 0)
    def _():
        gather_rows(refs[:count], sizes, grads)

    for j in range(tiles):

        @pl.when(step == j)
        def _():
            grad_hidden = dot_nt(grads[:rows, :], down_w[...])
            tile = grad_hidden.shape[1]
            for at, slope, out in ((0, gate_d, gate_out), (units, up_d, up_out)):
                value = (grad_hidden * slope[:rows, :].astype(F32)).astype(BF16)
                grad_pre[:, at + j * tile : at + (j + 1) * tile] = value[rows - capacity :, :]
                out[:rows, :] = value
                if rows < out.shape[0]:
                    out[rows:, :] = jnp.zeros((out.shape[0] - rows, tile), BF16)

    @pl.when(step >= tiles)
    def _():
        last[...] = dot_nt(grad_pre[...], w_ref[...]).astype(BF16)


def inner(group, sources, w_down, gate_d, up_d, w_pair, before):
    arrays, sizes = sum(sources, []), [len(s) for s in sources]
    capacity, width = min(a.shape[0] for a in arrays), arrays[0].shape[1]
    units = w_down.shape[0]
    tile = math.gcd(units, 256)
    tiles = units // tile
    block = min(width, 512)
    total, parts = parts_of(capacity, group)
    held, part = parts[not before]

    def tile_at(i):
        return jnp.minimum(i, tiles - 1)

    def block_at(i):
        return jnp.maximum(i - tiles, 0)

    first = len(arrays) + 4
    return pl.pallas_call(
        functools.partial(inner_kernel, sizes, len(sources) * capacity, tiles),
        grid=(tiles + width // block,),
        in_specs=[part_spec(a, capacity) for a in arrays]
        + [
            pl.BlockSpec((tile, width), lambda i: (tile_at(i), 0)),
            pl.BlockSpec((held, tile), lambda i: (0, tile_at(i))),
            pl.BlockSpec((held, tile), lambda i: (0, tile_at(i))),
            pl.BlockSpec((block, 2 * units), lambda i: (block_at(i), 0)),
        ]
        + [pl.BlockSpec(memory_space=pl.ANY) for _ in before],
        out_specs=[
            pl.BlockSpec((capacity, block), lambda i: (0, block_at(i))),
            pl.BlockSpec((held, width), lambda i: (part, 0)),
            pl.BlockSpec((held, tile), lambda i: (part, tile_at(i))),
            pl.BlockSpec((held, tile), lambda i: (part, tile_at(i))),
        ],
        out_shape=[
            jax.ShapeDtypeStruct((capacity, width), BF16),
            jax.ShapeDtypeStruct((total, width), BF16),
            jax.ShapeDtypeStruct((total, units), BF16),
            jax.ShapeDtypeStruct((total, units), BF16),
        ],
        scratch_shapes=[pltpu.VMEM((capacity, 2 * units), BF16)],
        input_output_aliases={first + i: 1 + i for i in range(len(before))},
        compiler_params=params(1, 20),
        cost_estimate=FREE,
        name="inner",
    )(*arrays, w_down, gate_d, up_d, w_pair, *before)


def back_kernel(sources, gate_ref, up_ref, w_ref, *outs):
    units, capacity = gate_ref.shape[1], outs[0].shape[0]
    rows = sources * capacity
    value = dot_nt(gate_ref[:rows, :], w_ref[:, :units])
    value += dot_nt(up_ref[:rows, :], w_ref[:, units:])
    for m, out in enumerate(outs):
        out[...] = value[m * capacity : (m + 1) * capacity, :].astype(BF16)


def back(group, capacity, gate, up, w_pair):
    width, units = w_pair.shape[0], gate.shape[1]
    held, part = parts_of(capacity, group)[1][False]
    sources = group - 2
    block = min(width, 512)
    return pl.pallas_call(
        functools.partial(back_kernel, sources),
        grid=(width // block,),
        in_specs=[
            pl.BlockSpec((held, units), lambda i: (part, 0)),
            pl.BlockSpec((held, units), lambda i: (part, 0)),
            pl.BlockSpec((block, 2 * units), lambda i: (i, 0)),
        ],
        out_specs=[pl.BlockSpec((capacity, block), lambda i: (0, i))] * sources,
        out_shape=[jax.ShapeDtypeStruct((capacity, width), BF16)] * sources,
        compiler_params=params(1, 18),
        cost_estimate=FREE,
        name="back",
    )(gate, up, w_pair)


def pair_chunks(flipped_rows, sides, chunk):
    for side in sides:
        for c in range(0, side.shape[1], chunk):
            yield dot(flipped_rows, side[:, c : c + chunk])


def lower_share(rows, chunk):
    return jnp.concatenate([rows[:, c : c + chunk] for c in range(0, rows.shape[1], chunk)], axis=0)


def hold_lower(which, shares, hidden_ref, rows, lower):
    own = hidden_ref.shape[1]
    stacked = jnp.concatenate(
        [hidden_ref[which(r)].astype(F32) for r in range(shares)], axis=0
    ).astype(BF16)
    lower[...] = dot(stacked, rows).reshape(shares, own, rows.shape[1])


def give_kernel(shares, chunk, which_ref, flip_ref, hidden_ref, grads, gate, up, out, lower):
    step = pl.program_id(0)

    @pl.when(step == 0)
    def _():
        hold_lower(lambda r: which_ref[r], shares, hidden_ref, grads[...], lower)

    at = 0
    for piece in pair_chunks(flip_ref[0], (gate[...], up[...]), chunk):
        out[0, at : at + piece.shape[0]] = piece.astype(BF16)
        at += piece.shape[0]
    out[0, at:] = lower_share(lower[step], chunk).astype(BF16)


def shared_operands(flipped, hidden, replicas):
    width, rows = flipped.shape
    units = hidden.shape[0]
    return (
        flipped.reshape(replicas, width // replicas, rows),
        hidden.reshape(replicas, units // replicas, rows),
    )


def give(which, flipped, hidden, grads, gate, up, replicas, chunk):
    rows, width = grads.shape
    units = gate.shape[1]
    shares = replicas // 2
    share_rows = (2 * units * (width // replicas) + (units // replicas) * width) // chunk
    flipped, hidden = shared_operands(flipped, hidden, replicas)
    return pl.pallas_call(
        functools.partial(give_kernel, shares, chunk),
        grid_spec=pltpu.PrefetchScalarGridSpec(
            num_scalar_prefetch=1,
            grid=(shares,),
            in_specs=[pl.BlockSpec((1, width // replicas, rows), lambda i, w: (w[i], 0, 0))]
            + [whole(a) for a in (hidden, grads, gate, up)],
            out_specs=pl.BlockSpec((1, share_rows, chunk), lambda i, w: (i, 0, 0)),
            scratch_shapes=[pltpu.VMEM((shares, units // replicas, width), F32)],
        ),
        out_shape=jax.ShapeDtypeStruct((shares, share_rows, chunk), BF16),
        compiler_params=params(1, 18),
        cost_estimate=FREE,
        name="give",
    )(which, flipped, hidden, grads, gate, up)


def split_kernel(shares, own, came, *outs):
    step = pl.program_id(0)
    total = own[0].astype(F32) + came[0].astype(F32)
    half = total.shape[0] // 2
    for r in range(shares):

        @pl.when(step == r)
        def _():
            outs[2 * r][...] = total[:half].astype(BF16)
            outs[2 * r + 1][...] = total[half:].astype(BF16)


def split(own, came):
    shares, share_rows, chunk = came.shape
    half = share_rows // 2
    share = pl.BlockSpec((1, share_rows, chunk), lambda i: (i, 0, 0))
    halves = pl.pallas_call(
        functools.partial(split_kernel, shares),
        grid=(shares,),
        in_specs=[share, share],
        out_specs=[pl.BlockSpec((half, chunk), lambda i: (0, 0))] * (2 * shares),
        out_shape=[jax.ShapeDtypeStruct((half, chunk), BF16)] * (2 * shares),
        compiler_params=params(1, 18),
        cost_estimate=FREE,
        name="split",
    )(own, came)
    return halves[::2], halves[1::2]


def halvings(shares, bits, before_last):
    terms = {r: [share] for r, share in enumerate(shares)}
    for bit in bits:
        pairs = [(i, i ^ (2 << bit)) for i in range(lax.axis_size("dp"))]
        for r in sorted((r for r in terms if (r >> bit) & 1), reverse=True):
            mine = terms.pop(r)
            if len(mine) > 1:
                mine = [sum(term.astype(F32) for term in mine).astype(BF16)]
            if bit == bits[-1]:
                mine = lax.optimization_barrier((mine[0], before_last))
            terms[r ^ (1 << bit)].append(lax.ppermute(mine[0], "dp", pairs))
    return terms[0]


def finish_kernel(count, chunk, *refs):
    halves, (pair, lower) = (refs[:count], refs[count : 2 * count]), refs[2 * count :]
    totals = []
    for terms in halves:
        total = terms[0][...].astype(F32)
        for term in terms[1:]:
            total += term[...].astype(F32)
        totals.append(total)
    half = totals[0].shape[0]
    at = 0
    for out in (pair, lower):
        rows, columns = out.shape
        for c in range(0, columns, chunk):
            cut = min(max(half - at, 0), rows)
            if cut:
                out[:cut, c : c + chunk] = totals[0][at : at + cut]
            if cut < rows:
                out[cut:, c : c + chunk] = totals[1][at + cut - half : at + rows - half]
            at += rows


def finish(firsts, seconds, pair_shape, lower_shape):
    chunk = firsts[0].shape[1]
    return pl.pallas_call(
        functools.partial(finish_kernel, len(firsts), chunk),
        grid=(1,),
        in_specs=[pl.BlockSpec(a.shape, lambda i: (0, 0)) for a in firsts + seconds],
        out_specs=[
            pl.BlockSpec(pair_shape, lambda i: (0, 0)),
            pl.BlockSpec(lower_shape, lambda i: (0, 0)),
        ],
        out_shape=[
            jax.ShapeDtypeStruct(pair_shape, F32),
            jax.ShapeDtypeStruct(lower_shape, F32),
        ],
        compiler_params=params(1, 24),
        cost_estimate=FREE,
        name="finish",
    )(*firsts, *seconds)


def local(tokens_in, out_grad, expert_ids, gate_weights, w_gate_up, w_down):
    tok_rows, width = tokens_in.shape
    top = expert_ids.shape[1]
    group = lax.axis_size("expert")
    replicas = lax.axis_size("dp")
    units = w_down.shape[1]
    capacity = 5 * tok_rows * top // (4 * group)
    chunk = math.gcd(units, width)
    me = lax.axis_index("expert").astype(jnp.int32)
    replica = lax.axis_index("dp").astype(jnp.int32)
    place = me.reshape(1)
    meta = pieces_of(expert_ids, gate_weights)
    w_pair, w_lower = w_gate_up[0], w_down[0]

    def move(array, pairs):
        return lax.ppermute(array, "expert", pairs)

    def swap(array, m):
        return move(array, [(i, i ^ m) for i in range(group)])

    def after(array, *others):
        return lax.optimization_barrier((array, *others))[0]

    if group == 4 and tok_rows < 2 * capacity:
        far, near, cross = [(0, 2), (3, 1)], [(1, 2), (2, 1)], [(1, 3), (2, 0)]
        far_rows, far_meta = move(tokens_in, far), move(meta, far)
        x0, g0, x1, g1, x2, g2, x3, g3 = pack(
            place, meta, dict(tokens=tokens_in, grads=out_grad), [0, 1, 2, 3], [], capacity, top
        )
        x1, x3, x2 = swap(x1, 1), move(after(x3, far_meta), near), move(x2, cross)
        cx, onward = pack(place, far_meta, dict(tokens=far_rows), [0, 1], [], capacity + 16, top)
        onward = move(onward, [(2, 3), (1, 0)])
        g1 = swap(after(g1, x1), 1)
        g2 = swap(after(g2, x3), 2)
        g3 = swap(after(g3, x2), 3)
        inputs, grads = [[x0], [x1], [cx, x2], [onward, x3]], [[g0], [g1], [g2], [g3]]
    else:
        offsets = list(range(group))
        packed = pack(
            place, meta, dict(tokens=tokens_in, grads=out_grad), offsets, [], capacity, top
        )
        moved = [packed[2 * m : 2 * m + 2] for m in offsets]
        moved = [moved[0]] + [[swap(a, m) for a in moved[m]] for m in offsets[1:]]
        inputs, grads = [[a] for a, _ in moved], [[b] for _, b in moved]

    own_d = forward(group, inputs[:1], w_pair, [])
    others_d = forward(group, inputs[1:], w_pair, own_d[2:])
    own_back, *own_grads = inner(group, grads[:1], w_lower, *own_d[:2], w_pair, [])
    last, *late = inner(group, grads[1:], w_lower, *others_d[:2], w_pair, own_grads)
    returned = [own_back, *back(group, capacity, *late[1:], w_pair), last]
    for m in range(group - 1, 0, -1):
        ahead = returned[m + 1 :] if 2 * m >= group else []
        returned[m] = swap(after(returned[m], *ahead), m)

    shares = replicas // 2
    own = [replica ^ (2 * r) for r in range(shares)]
    operands = (others_d[3], others_d[2], *late)
    first_own = jnp.stack(own) ^ 1
    given = give(first_own, *operands, replicas, chunk)
    came = lax.ppermute(given, "dp", [(i, i ^ 1) for i in range(replicas)])
    mine = give(after(jnp.stack(own), given), *operands, replicas, chunk)
    bits = list(range(shares.bit_length() - 1))
    middle = len(bits) // 2
    first_bits, second_bits = bits, bits[middle:] + bits[:middle]
    first, second = split(mine, came)
    ahead = (returned[1], returned[-1])
    firsts = halvings(first, first_bits, ahead)
    seconds = halvings(second, second_bits, ahead)
    pair_sum, lower_sum = finish(
        firsts, seconds, (width // replicas, 2 * units), (units // replicas, width)
    )
    *returned, pair_sum, lower_sum = lax.optimization_barrier((*returned, pair_sum, lower_sum))
    grad_tokens = combine(place, meta, returned, top)
    return (grad_tokens, pair_sum, lower_sum)


def solution(mesh):
    in_specs = (
        P(("dp", "expert"), None),
        P(("dp", "expert"), None),
        P(("dp", "expert"), None),
        P(("dp", "expert"), None),
        P("expert", None, None),
        P("expert", None, None),
    )
    out_specs = (P(("dp", "expert"), None), P("dp", "expert"), P("dp", "expert"))
    return jax.shard_map(local, mesh=mesh, in_specs=in_specs, out_specs=out_specs, check_vma=False)
```

```python
import functools
import math

import jax
import jax.numpy as jnp
from jax import lax
from jax.experimental import pallas as pl
from jax.experimental.pallas import tpu as pltpu
from jax.sharding import PartitionSpec as P

F32 = jnp.float32
BF16 = jnp.bfloat16
MIB = 1024 * 1024


def params(grid_rank, mebibytes):
    return pltpu.CompilerParams(
        dimension_semantics=("arbitrary",) * grid_rank, vmem_limit_bytes=mebibytes * MIB
    )


def cost(macs):
    return pl.CostEstimate(flops=2 * macs, bytes_accessed=1, transcendentals=0)


FREE = pl.CostEstimate(flops=1, bytes_accessed=1, transcendentals=0)


def whole(array):
    rank = array.ndim
    return pl.BlockSpec(
        array.shape, lambda *at: (0,) * rank, pipeline_mode=pl.Buffered(buffer_count=1)
    )


def dot(a, b):
    return lax.dot_general(a, b, (((1,), (0,)), ((), ())), preferred_element_type=F32)


def dot_nt(a, b):
    return lax.dot_general(a, b, (((1,), (1,)), ((), ())), preferred_element_type=F32)


def pick_matrices(me, ids, offsets, capacity):
    top, rows = ids.shape
    lines = max(8, max(offsets) + 1)
    wanted = (lax.broadcasted_iota(jnp.int32, (lines, rows), 0) ^ me).astype(F32)
    named = ids[0:1, :] == wanted
    for k in range(1, top):
        named = named | (ids[k : k + 1, :] == wanted)
    named = named.astype(F32)
    before = lax.broadcasted_iota(jnp.int32, (rows, rows), 0) <= lax.broadcasted_iota(
        jnp.int32, (rows, rows), 1
    )
    place = dot(named.astype(BF16), before.astype(F32).astype(BF16))
    place = jnp.where(named > 0, place - 1.0, -1.0)
    slots = lax.broadcasted_iota(jnp.int32, (capacity, rows), 0).astype(F32)
    return [(place[m : m + 1, :] == slots).astype(F32) for m in offsets]


def pieces_of(ids, gates):
    lines, rest = [ids.T.astype(BF16)], gates.T
    for _ in range(3):
        term = lax.reduce_precision(rest, 8, 7)
        lines.append(term.astype(BF16))
        rest = rest - term
    lines = jnp.concatenate(lines, axis=0)
    return jnp.pad(lines, ((0, -lines.shape[0] % 16), (0, 0)))


def ids_and_gates(meta, top):
    meta = meta.astype(F32)
    terms = [meta[top * (1 + i) : top * (2 + i)] for i in range(3)]
    return meta[:top], (terms[2] + terms[1]) + terms[0]


def pack_kernel(offsets, joint, top, kinds, me_ref, meta_ref, *rest):
    sources, outs, (pick, gain) = rest[: len(kinds)], list(rest[len(kinds) : -2]), rest[-2:]
    capacity = pick.shape[1]

    @pl.when(pl.program_id(0) == 0)
    def _():
        me = me_ref[0]
        ids, gates = ids_and_gates(meta_ref[...], top)
        for at, matrix in enumerate(pick_matrices(me, ids, offsets, capacity)):
            pick[at] = matrix.astype(BF16)
            chosen = jnp.where(ids == (me ^ offsets[at]).astype(F32), gates, 0.0)
            weight = jnp.sum(chosen, axis=0, keepdims=True)
            gain[at] = jnp.broadcast_to(
                jnp.sum(matrix * weight, axis=1, keepdims=True), gain.shape[1:]
            )

    for at, m in enumerate(offsets):
        out = outs.pop(0) if m in joint else None
        for which, (kind, source) in enumerate(zip(kinds, sources, strict=True)):
            rows = dot(pick[at], source[...])
            if kind == "grads":
                rows = rows * gain[at][:, 0:1]
            if out is None:
                outs.pop(0)[...] = rows.astype(BF16)
            else:
                out[which] = rows.astype(BF16)


def pack(me, meta, sources, offsets, joint, capacity, top):
    rows, width = next(iter(sources.values())).shape
    block = min(width, 512)
    count = len(offsets)
    out_specs, out_shape = [], []
    for m in offsets:
        if m in joint:
            lead = len(sources)
            out_specs.append(pl.BlockSpec((lead, capacity, block), lambda i: (0, 0, i)))
            out_shape.append(jax.ShapeDtypeStruct((lead, capacity, width), BF16))
        else:
            out_specs += [pl.BlockSpec((capacity, block), lambda i: (0, i))] * len(sources)
            out_shape += [jax.ShapeDtypeStruct((capacity, width), BF16)] * len(sources)
    return pl.pallas_call(
        functools.partial(pack_kernel, offsets, joint, top, list(sources)),
        grid=(width // block,),
        in_specs=[
            pl.BlockSpec(memory_space=pltpu.SMEM),
            pl.BlockSpec(meta.shape, lambda i: (0, 0)),
        ]
        + [pl.BlockSpec((rows, block), lambda i: (0, i))] * len(sources),
        out_specs=out_specs,
        out_shape=out_shape,
        scratch_shapes=[
            pltpu.VMEM((count, capacity, rows), BF16),
            pltpu.VMEM((count, capacity, 128), F32),
        ],
        compiler_params=params(1, 14),
        cost_estimate=FREE,
        name="pack",
    )(me, meta, *sources.values())


def combine_kernel(offsets, top, me_ref, meta_ref, *refs):
    count = len(offsets)
    blocks, total_ref, last_pick, pick = refs[: count - 1], refs[-3], refs[-2], refs[-1]

    @pl.when(pl.program_id(0) == 0)
    def _():
        ids, _ = ids_and_gates(meta_ref[...], top)
        matrices = pick_matrices(me_ref[0], ids, offsets, last_pick.shape[1])
        for at, matrix in enumerate(matrices[:-1]):
            pick[at] = matrix.T.astype(BF16)
        last_pick[...] = matrices[-1].T.astype(BF16)

    total = dot(pick[0], blocks[0][...])
    for at in range(1, count - 1):
        total += dot(pick[at], blocks[at][...])
    total_ref[...] = total


def combine(me, meta, blocks, offsets, top):
    capacity, width = blocks[0].shape
    rows, count = meta.shape[1], len(offsets)
    block = min(width, 512)
    return pl.pallas_call(
        functools.partial(combine_kernel, offsets, top),
        grid=(width // block,),
        in_specs=[
            pl.BlockSpec(memory_space=pltpu.SMEM),
            pl.BlockSpec(meta.shape, lambda i: (0, 0)),
        ]
        + [pl.BlockSpec((capacity, block), lambda i: (0, i))] * (count - 1),
        out_specs=[
            pl.BlockSpec((rows, block), lambda i: (0, i)),
            pl.BlockSpec((rows, capacity), lambda i: (0, 0)),
        ],
        out_shape=[
            jax.ShapeDtypeStruct((rows, width), F32),
            jax.ShapeDtypeStruct((rows, capacity), BF16),
        ],
        scratch_shapes=[pltpu.VMEM((count - 1, rows, capacity), BF16)],
        compiler_params=params(1, 10),
        cost_estimate=FREE,
        name="combine",
    )(me, meta, *blocks)


def last_sum_kernel(total, pick, block, out):
    out[...] = (total[...] + dot(pick[...], block[...])).astype(BF16)


def last_sum(total, pick, rows):
    tokens, width = total.shape
    block = min(width, 1024)
    return pl.pallas_call(
        last_sum_kernel,
        grid=(width // block,),
        in_specs=[
            pl.BlockSpec((tokens, block), lambda i: (0, i)),
            pl.BlockSpec(pick.shape, lambda i: (0, 0)),
            pl.BlockSpec((rows.shape[0], block), lambda i: (0, i)),
        ],
        out_specs=pl.BlockSpec((tokens, block), lambda i: (0, i)),
        out_shape=jax.ShapeDtypeStruct((tokens, width), BF16),
        compiler_params=params(1, 10),
        cost_estimate=FREE,
        name="last_sum",
    )(total, pick, rows)


def parts_of(capacity, group):
    own = -(-capacity // 128) * 128
    others = -(-(group - 1) * capacity // own) * own
    return own + others, {True: (own, others // own), False: (others, 0)}


def gather_rows(parts, sizes, held):
    at, parts = 0, list(parts)
    for size in sizes:
        mine, parts = parts[:size], parts[size:]
        rows = mine[0][...]
        for other in mine[1:]:
            rows = rows + other[...]
        held[at : at + rows.shape[0], :] = rows
        at += rows.shape[0]
    if at < held.shape[0]:
        held[at:, :] = jnp.zeros((held.shape[0] - at, held.shape[1]), held.dtype)


def part_spec(array, capacity):
    block = (capacity, array.shape[1])
    return pl.BlockSpec(block, lambda i: (0, 0), pipeline_mode=pl.Buffered(buffer_count=1))


def forward_kernel(sizes, *refs):
    count = sum(sizes)
    gate_w, up_w = refs[count : count + 2]
    gate_out, up_out, hidden_out, flipped, held = refs[-5:]

    @pl.when(pl.program_id(0) == 0)
    def _():
        gather_rows(refs[:count], sizes, held)
        step = min(held.shape[1], 256)
        for d in range(0, held.shape[1], step):
            flipped[d : d + step, :] = held[:, d : d + step].T

    gate, up = dot(held[...], gate_w[...]), dot(held[...], up_w[...])
    sigmoid = jax.nn.sigmoid(gate)
    swish = gate * sigmoid
    gate_out[...] = (up * sigmoid * (1.0 + gate * (1.0 - sigmoid))).astype(BF16)
    up_out[...] = swish.astype(BF16)
    hidden_out[...] = (swish * up).T.astype(BF16)


def forward(group, sources, w_pair, before):
    arrays, sizes = sum(sources, []), [len(s) for s in sources]
    capacity, width = min(a.shape[0] for a in arrays), arrays[0].shape[1]
    units = w_pair.shape[1] // 2
    tile = math.gcd(units, 256)
    tiles = units // tile
    total, parts = parts_of(capacity, group)
    rows, part = parts[not before]
    shapes = [
        jax.ShapeDtypeStruct((rows, units), BF16),
        jax.ShapeDtypeStruct((rows, units), BF16),
        jax.ShapeDtypeStruct((units, total), BF16),
        jax.ShapeDtypeStruct((width, total), BF16),
    ]
    first = len(arrays) + 2
    return pl.pallas_call(
        functools.partial(forward_kernel, sizes),
        grid=(tiles,),
        in_specs=[part_spec(a, capacity) for a in arrays]
        + [
            pl.BlockSpec((width, tile), lambda j: (0, j)),
            pl.BlockSpec((width, tile), lambda j: (0, tiles + j)),
        ]
        + [pl.BlockSpec(memory_space=pl.ANY) for _ in before],
        out_specs=[
            pl.BlockSpec((rows, tile), lambda j: (0, j)),
            pl.BlockSpec((rows, tile), lambda j: (0, j)),
            pl.BlockSpec((tile, rows), lambda j: (j, part)),
            pl.BlockSpec((width, rows), lambda j: (0, part)),
        ],
        out_shape=shapes,
        scratch_shapes=[pltpu.VMEM((rows, width), BF16)],
        input_output_aliases={first + i: 2 + i for i in range(len(before))},
        compiler_params=params(1, 20),
        cost_estimate=cost(rows * width * units),
        name="forward",
    )(*arrays, w_pair, w_pair, *before)


def inner_kernel(sizes, rows, tiles, *refs):
    count = sum(sizes)
    down_w, gate_d, up_d, w_ref = refs[count : count + 4]
    last, grads, gate_out, up_out, grad_pre = refs[-5:]
    step = pl.program_id(0)
    units, capacity = grad_pre.shape[1] // 2, last.shape[0]

    @pl.when(step == 0)
    def _():
        gather_rows(refs[:count], sizes, grads)

    for j in range(tiles):

        @pl.when(step == j)
        def _():
            grad_hidden = dot_nt(grads[:rows, :], down_w[...])
            tile = grad_hidden.shape[1]
            for at, slope, out in ((0, gate_d, gate_out), (units, up_d, up_out)):
                value = (grad_hidden * slope[:rows, :].astype(F32)).astype(BF16)
                grad_pre[:, at + j * tile : at + (j + 1) * tile] = value[rows - capacity :, :]
                out[:rows, :] = value
                if rows < out.shape[0]:
                    out[rows:, :] = jnp.zeros((out.shape[0] - rows, tile), BF16)

    @pl.when(step >= tiles)
    def _():
        last[...] = dot_nt(grad_pre[...], w_ref[...]).astype(BF16)


def inner(group, sources, w_down, gate_d, up_d, w_pair, before):
    arrays, sizes = sum(sources, []), [len(s) for s in sources]
    capacity, width = min(a.shape[0] for a in arrays), arrays[0].shape[1]
    units = w_down.shape[0]
    tile = math.gcd(units, 256)
    tiles = units // tile
    block = min(width, 512)
    total, parts = parts_of(capacity, group)
    held, part = parts[not before]

    def tile_at(i):
        return jnp.minimum(i, tiles - 1)

    def block_at(i):
        return jnp.maximum(i - tiles, 0)

    first = len(arrays) + 4
    return pl.pallas_call(
        functools.partial(inner_kernel, sizes, len(sources) * capacity, tiles),
        grid=(tiles + width // block,),
        in_specs=[part_spec(a, capacity) for a in arrays]
        + [
            pl.BlockSpec((tile, width), lambda i: (tile_at(i), 0)),
            pl.BlockSpec((held, tile), lambda i: (0, tile_at(i))),
            pl.BlockSpec((held, tile), lambda i: (0, tile_at(i))),
            pl.BlockSpec((block, 2 * units), lambda i: (block_at(i), 0)),
        ]
        + [pl.BlockSpec(memory_space=pl.ANY) for _ in before],
        out_specs=[
            pl.BlockSpec((capacity, block), lambda i: (0, block_at(i))),
            pl.BlockSpec((held, width), lambda i: (part, 0)),
            pl.BlockSpec((held, tile), lambda i: (part, tile_at(i))),
            pl.BlockSpec((held, tile), lambda i: (part, tile_at(i))),
        ],
        out_shape=[
            jax.ShapeDtypeStruct((capacity, width), BF16),
            jax.ShapeDtypeStruct((total, width), BF16),
            jax.ShapeDtypeStruct((total, units), BF16),
            jax.ShapeDtypeStruct((total, units), BF16),
        ],
        scratch_shapes=[pltpu.VMEM((capacity, 2 * units), BF16)],
        input_output_aliases={first + i: 1 + i for i in range(len(before))},
        compiler_params=params(1, 20),
        cost_estimate=FREE,
        name="inner",
    )(*arrays, w_down, gate_d, up_d, w_pair, *before)


def back_kernel(sources, gate_ref, up_ref, w_ref, *outs):
    units, capacity = gate_ref.shape[1], outs[0].shape[0]
    rows = sources * capacity
    value = dot_nt(gate_ref[:rows, :], w_ref[:, :units])
    value += dot_nt(up_ref[:rows, :], w_ref[:, units:])
    for m, out in enumerate(outs):
        out[...] = value[m * capacity : (m + 1) * capacity, :].astype(BF16)


def back(group, capacity, gate, up, w_pair):
    width, units = w_pair.shape[0], gate.shape[1]
    held, part = parts_of(capacity, group)[1][False]
    sources = group - 2
    block = min(width, 512)
    return pl.pallas_call(
        functools.partial(back_kernel, sources),
        grid=(width // block,),
        in_specs=[
            pl.BlockSpec((held, units), lambda i: (part, 0)),
            pl.BlockSpec((held, units), lambda i: (part, 0)),
            pl.BlockSpec((block, 2 * units), lambda i: (i, 0)),
        ],
        out_specs=[pl.BlockSpec((capacity, block), lambda i: (0, i))] * sources,
        out_shape=[jax.ShapeDtypeStruct((capacity, width), BF16)] * sources,
        compiler_params=params(1, 18),
        cost_estimate=FREE,
        name="back",
    )(gate, up, w_pair)


def pair_chunks(flipped_rows, sides, chunk):
    for side in sides:
        for c in range(0, side.shape[1], chunk):
            yield dot(flipped_rows, side[:, c : c + chunk])


def lower_share(rows, chunk):
    return jnp.concatenate([rows[:, c : c + chunk] for c in range(0, rows.shape[1], chunk)], axis=0)


def hold_lower(which, shares, hidden_ref, rows, lower):
    own = hidden_ref.shape[1]
    stacked = jnp.concatenate(
        [hidden_ref[which(r)].astype(F32) for r in range(shares)], axis=0
    ).astype(BF16)
    lower[...] = dot(stacked, rows).reshape(shares, own, rows.shape[1])


def give_kernel(shares, chunk, which_ref, flip_ref, hidden_ref, grads, gate, up, out, lower):
    step = pl.program_id(0)

    @pl.when(step == 0)
    def _():
        hold_lower(lambda r: which_ref[r], shares, hidden_ref, grads[...], lower)

    at = 0
    for piece in pair_chunks(flip_ref[0], (gate[...], up[...]), chunk):
        out[0, at : at + piece.shape[0]] = piece.astype(BF16)
        at += piece.shape[0]
    out[0, at:] = lower_share(lower[step], chunk).astype(BF16)


def shared_operands(flipped, hidden, replicas):
    width, rows = flipped.shape
    units = hidden.shape[0]
    return (
        flipped.reshape(replicas, width // replicas, rows),
        hidden.reshape(replicas, units // replicas, rows),
    )


def give(which, flipped, hidden, grads, gate, up, replicas, chunk):
    rows, width = grads.shape
    units = gate.shape[1]
    shares = replicas // 2
    share_rows = (2 * units * (width // replicas) + (units // replicas) * width) // chunk
    flipped, hidden = shared_operands(flipped, hidden, replicas)
    return pl.pallas_call(
        functools.partial(give_kernel, shares, chunk),
        grid_spec=pltpu.PrefetchScalarGridSpec(
            num_scalar_prefetch=1,
            grid=(shares,),
            in_specs=[pl.BlockSpec((1, width // replicas, rows), lambda i, w: (w[i], 0, 0))]
            + [whole(a) for a in (hidden, grads, gate, up)],
            out_specs=pl.BlockSpec((1, share_rows, chunk), lambda i, w: (i, 0, 0)),
            scratch_shapes=[pltpu.VMEM((shares, units // replicas, width), F32)],
        ),
        out_shape=jax.ShapeDtypeStruct((shares, share_rows, chunk), BF16),
        compiler_params=params(1, 18),
        cost_estimate=FREE,
        name="give",
    )(which, flipped, hidden, grads, gate, up)


def split_kernel(shares, own, came, *outs):
    step = pl.program_id(0)
    total = own[0].astype(F32) + came[0].astype(F32)
    half = total.shape[0] // 2
    for r in range(shares):

        @pl.when(step == r)
        def _():
            outs[2 * r][...] = total[:half].astype(BF16)
            outs[2 * r + 1][...] = total[half:].astype(BF16)


def split(own, came):
    shares, share_rows, chunk = came.shape
    half = share_rows // 2
    share = pl.BlockSpec((1, share_rows, chunk), lambda i: (i, 0, 0))
    halves = pl.pallas_call(
        functools.partial(split_kernel, shares),
        grid=(shares,),
        in_specs=[share, share],
        out_specs=[pl.BlockSpec((half, chunk), lambda i: (0, 0))] * (2 * shares),
        out_shape=[jax.ShapeDtypeStruct((half, chunk), BF16)] * (2 * shares),
        compiler_params=params(1, 18),
        cost_estimate=FREE,
        name="split",
    )(own, came)
    return halves[::2], halves[1::2]


def halvings(shares, bits, before_last):
    terms = {r: [share] for r, share in enumerate(shares)}
    for bit in bits:
        pairs = [(i, i ^ (2 << bit)) for i in range(lax.axis_size("dp"))]
        for r in sorted((r for r in terms if (r >> bit) & 1), reverse=True):
            mine = terms.pop(r)
            if len(mine) > 1:
                mine = [sum(term.astype(F32) for term in mine).astype(BF16)]
            if bit == bits[-1]:
                mine = lax.optimization_barrier((mine[0], before_last))
            terms[r ^ (1 << bit)].append(lax.ppermute(mine[0], "dp", pairs))
    return terms[0]


def finish_kernel(count, chunk, *refs):
    halves, (pair, lower) = (refs[:count], refs[count : 2 * count]), refs[2 * count :]
    totals = []
    for terms in halves:
        total = terms[0][...].astype(F32)
        for term in terms[1:]:
            total += term[...].astype(F32)
        totals.append(total)
    half = totals[0].shape[0]
    at = 0
    for out in (pair, lower):
        rows, columns = out.shape
        for c in range(0, columns, chunk):
            cut = min(max(half - at, 0), rows)
            if cut:
                out[:cut, c : c + chunk] = totals[0][at : at + cut]
            if cut < rows:
                out[cut:, c : c + chunk] = totals[1][at + cut - half : at + rows - half]
            at += rows


def finish(firsts, seconds, pair_shape, lower_shape):
    chunk = firsts[0].shape[1]
    return pl.pallas_call(
        functools.partial(finish_kernel, len(firsts), chunk),
        grid=(1,),
        in_specs=[pl.BlockSpec(a.shape, lambda i: (0, 0)) for a in firsts + seconds],
        out_specs=[
            pl.BlockSpec(pair_shape, lambda i: (0, 0)),
            pl.BlockSpec(lower_shape, lambda i: (0, 0)),
        ],
        out_shape=[
            jax.ShapeDtypeStruct(pair_shape, F32),
            jax.ShapeDtypeStruct(lower_shape, F32),
        ],
        compiler_params=params(1, 24),
        cost_estimate=FREE,
        name="finish",
    )(*firsts, *seconds)


def local(tokens_in, out_grad, expert_ids, gate_weights, w_gate_up, w_down):
    tok_rows, width = tokens_in.shape
    top = expert_ids.shape[1]
    group = lax.axis_size("expert")
    replicas = lax.axis_size("dp")
    units = w_down.shape[1]
    capacity = 5 * tok_rows * top // (4 * group)
    chunk = math.gcd(units, width)
    me = lax.axis_index("expert").astype(jnp.int32)
    replica = lax.axis_index("dp").astype(jnp.int32)
    place = me.reshape(1)
    meta = pieces_of(expert_ids, gate_weights)
    w_pair, w_lower = w_gate_up[0], w_down[0]

    def move(array, pairs):
        return lax.ppermute(array, "expert", pairs)

    def swap(array, m):
        return move(array, [(i, i ^ m) for i in range(group)])

    def after(array, *others):
        return lax.optimization_barrier((array, *others))[0]

    if group == 4 and tok_rows < 2 * capacity:
        far, near, cross = [(0, 2), (3, 1)], [(1, 2), (2, 1)], [(1, 3), (2, 0)]
        far_rows, far_meta = move(tokens_in, far), move(meta, far)
        x0, g0, x1, g1, x2, g2, x3, g3 = pack(
            place, meta, dict(tokens=tokens_in, grads=out_grad), [0, 1, 2, 3], [], capacity, top
        )
        x1, x3, x2 = swap(x1, 1), move(after(x3, far_meta), near), move(x2, cross)
        cx, onward = pack(place, far_meta, dict(tokens=far_rows), [0, 1], [], capacity + 16, top)
        onward = move(onward, [(2, 3), (1, 0)])
        g1 = swap(after(g1, x1), 1)
        g2 = swap(after(g2, x3), 2)
        g3 = swap(after(g3, x2), 3)
        inputs, grads = [[x0], [x1], [cx, x2], [onward, x3]], [[g0], [g1], [g2], [g3]]
    else:
        offsets = list(range(group))
        packed = pack(
            place, meta, dict(tokens=tokens_in, grads=out_grad), offsets, [], capacity, top
        )
        moved = [packed[2 * m : 2 * m + 2] for m in offsets]
        moved = [moved[0]] + [[swap(a, m) for a in moved[m]] for m in offsets[1:]]
        inputs, grads = [[a] for a, _ in moved], [[b] for _, b in moved]

    own_d = forward(group, inputs[:1], w_pair, [])
    others_d = forward(group, inputs[1:], w_pair, own_d[2:])
    own_back, *own_grads = inner(group, grads[:1], w_lower, *own_d[:2], w_pair, [])
    last, *late = inner(group, grads[1:], w_lower, *others_d[:2], w_pair, own_grads)
    returned = [own_back, *back(group, capacity, *late[1:], w_pair), last]
    for m in range(group - 1, 0, -1):
        ahead = returned[m + 1 :] if 2 * m >= group else []
        returned[m] = swap(after(returned[m], *ahead), m)

    shares = replicas // 2
    own = [replica ^ (2 * r) for r in range(shares)]
    operands = (others_d[3], others_d[2], *late)
    first_own = jnp.stack(own) ^ 1
    given = give(first_own, *operands, replicas, chunk)
    came = lax.ppermute(given, "dp", [(i, i ^ 1) for i in range(replicas)])
    mine = give(after(jnp.stack(own), given), *operands, replicas, chunk)
    bits = list(range(shares.bit_length() - 1))
    middle = len(bits) // 2
    first_bits, second_bits = bits, bits[middle:] + bits[:middle]
    first, second = split(mine, came)
    ahead = (returned[1], returned[-1])
    firsts = halvings(first, first_bits, ahead)
    seconds = halvings(second, second_bits, ahead)
    latest = max(1, group // 2)
    offsets = [m for m in range(group) if m != latest] + [latest]
    soon = [returned[m] for m in offsets[:-1]]
    soon, firsts[1], seconds[1] = lax.optimization_barrier((soon, firsts[1], seconds[1]))
    total, pick = combine(place, meta, soon, offsets, top)
    pair_sum, lower_sum = finish(
        firsts, seconds, (width // replicas, 2 * units), (units // replicas, width)
    )
    late_rows, pair_sum, lower_sum, total = lax.optimization_barrier(
        (returned[latest], pair_sum, lower_sum, total)
    )
    grad_tokens = last_sum(total, pick, late_rows)
    return (grad_tokens, pair_sum, lower_sum)


def solution(mesh):
    in_specs = (
        P(("dp", "expert"), None),
        P(("dp", "expert"), None),
        P(("dp", "expert"), None),
        P(("dp", "expert"), None),
        P("expert", None, None),
        P("expert", None, None),
    )
    out_specs = (P(("dp", "expert"), None), P("dp", "expert"), P("dp", "expert"))
    return jax.shard_map(local, mesh=mesh, in_specs=in_specs, out_specs=out_specs, check_vma=False)
```

```python
import functools
import math

import jax
import jax.numpy as jnp
from jax import lax
from jax.experimental import pallas as pl
from jax.experimental.pallas import tpu as pltpu
from jax.sharding import PartitionSpec as P

F32 = jnp.float32
BF16 = jnp.bfloat16
MIB = 1024 * 1024


def params(grid_rank, mebibytes):
    return pltpu.CompilerParams(
        dimension_semantics=("arbitrary",) * grid_rank, vmem_limit_bytes=mebibytes * MIB
    )


def cost(macs):
    return pl.CostEstimate(flops=2 * macs, bytes_accessed=1, transcendentals=0)


FREE = pl.CostEstimate(flops=1, bytes_accessed=1, transcendentals=0)


def whole(array):
    rank = array.ndim
    return pl.BlockSpec(
        array.shape, lambda *at: (0,) * rank, pipeline_mode=pl.Buffered(buffer_count=1)
    )


def dot(a, b):
    return lax.dot_general(a, b, (((1,), (0,)), ((), ())), preferred_element_type=F32)


def dot_nt(a, b):
    return lax.dot_general(a, b, (((1,), (1,)), ((), ())), preferred_element_type=F32)


def pick_matrices(me, ids, offsets, capacity):
    top, rows = ids.shape
    lines = max(8, max(offsets) + 1)
    wanted = (lax.broadcasted_iota(jnp.int32, (lines, rows), 0) ^ me).astype(F32)
    named = ids[0:1, :] == wanted
    for k in range(1, top):
        named = named | (ids[k : k + 1, :] == wanted)
    named = named.astype(F32)
    before = lax.broadcasted_iota(jnp.int32, (rows, rows), 0) <= lax.broadcasted_iota(
        jnp.int32, (rows, rows), 1
    )
    place = dot(named.astype(BF16), before.astype(F32).astype(BF16))
    place = jnp.where(named > 0, place - 1.0, -1.0)
    slots = lax.broadcasted_iota(jnp.int32, (capacity, rows), 0).astype(F32)
    return [(place[m : m + 1, :] == slots).astype(F32) for m in offsets]


def pieces_of(ids, gates):
    lines, rest = [ids.T.astype(BF16)], gates.T
    for _ in range(3):
        term = lax.reduce_precision(rest, 8, 7)
        lines.append(term.astype(BF16))
        rest = rest - term
    lines = jnp.concatenate(lines, axis=0)
    return jnp.pad(lines, ((0, -lines.shape[0] % 16), (0, 0)))


def ids_and_gates(meta, top):
    meta = meta.astype(F32)
    terms = [meta[top * (1 + i) : top * (2 + i)] for i in range(3)]
    return meta[:top], (terms[2] + terms[1]) + terms[0]


def pack_kernel(offsets, joint, top, kinds, me_ref, meta_ref, *rest):
    sources, outs, (pick, gain) = rest[: len(kinds)], list(rest[len(kinds) : -2]), rest[-2:]
    capacity = pick.shape[1]

    @pl.when(pl.program_id(0) == 0)
    def _():
        me = me_ref[0]
        ids, gates = ids_and_gates(meta_ref[...], top)
        for at, matrix in enumerate(pick_matrices(me, ids, offsets, capacity)):
            pick[at] = matrix.astype(BF16)
            chosen = jnp.where(ids == (me ^ offsets[at]).astype(F32), gates, 0.0)
            weight = jnp.sum(chosen, axis=0, keepdims=True)
            gain[at] = jnp.broadcast_to(
                jnp.sum(matrix * weight, axis=1, keepdims=True), gain.shape[1:]
            )

    for at, m in enumerate(offsets):
        out = outs.pop(0) if m in joint else None
        for which, (kind, source) in enumerate(zip(kinds, sources, strict=True)):
            rows = dot(pick[at], source[...])
            if kind == "grads":
                rows = rows * gain[at][:, 0:1]
            if out is None:
                outs.pop(0)[...] = rows.astype(BF16)
            else:
                out[which] = rows.astype(BF16)


def pack(me, meta, sources, offsets, joint, capacity, top):
    rows, width = next(iter(sources.values())).shape
    block = min(width, 512)
    count = len(offsets)
    out_specs, out_shape = [], []
    for m in offsets:
        if m in joint:
            lead = len(sources)
            out_specs.append(pl.BlockSpec((lead, capacity, block), lambda i: (0, 0, i)))
            out_shape.append(jax.ShapeDtypeStruct((lead, capacity, width), BF16))
        else:
            out_specs += [pl.BlockSpec((capacity, block), lambda i: (0, i))] * len(sources)
            out_shape += [jax.ShapeDtypeStruct((capacity, width), BF16)] * len(sources)
    return pl.pallas_call(
        functools.partial(pack_kernel, offsets, joint, top, list(sources)),
        grid=(width // block,),
        in_specs=[
            pl.BlockSpec(memory_space=pltpu.SMEM),
            pl.BlockSpec(meta.shape, lambda i: (0, 0)),
        ]
        + [pl.BlockSpec((rows, block), lambda i: (0, i))] * len(sources),
        out_specs=out_specs,
        out_shape=out_shape,
        scratch_shapes=[
            pltpu.VMEM((count, capacity, rows), BF16),
            pltpu.VMEM((count, capacity, 128), F32),
        ],
        compiler_params=params(1, 14),
        cost_estimate=FREE,
        name="pack",
    )(me, meta, *sources.values())


def combine_kernel(offsets, top, me_ref, meta_ref, *refs):
    count = len(offsets)
    blocks, total_ref, last_pick, pick = refs[: count - 1], refs[-3], refs[-2], refs[-1]

    @pl.when(pl.program_id(0) == 0)
    def _():
        ids, _ = ids_and_gates(meta_ref[...], top)
        matrices = pick_matrices(me_ref[0], ids, offsets, last_pick.shape[1])
        for at, matrix in enumerate(matrices[:-1]):
            pick[at] = matrix.T.astype(BF16)
        last_pick[...] = matrices[-1].T.astype(BF16)

    total = dot(pick[0], blocks[0][...])
    for at in range(1, count - 1):
        total += dot(pick[at], blocks[at][...])
    total_ref[...] = total


def combine(me, meta, blocks, offsets, top):
    capacity, width = blocks[0].shape
    rows, count = meta.shape[1], len(offsets)
    block = min(width, 512)
    return pl.pallas_call(
        functools.partial(combine_kernel, offsets, top),
        grid=(width // block,),
        in_specs=[
            pl.BlockSpec(memory_space=pltpu.SMEM),
            pl.BlockSpec(meta.shape, lambda i: (0, 0)),
        ]
        + [pl.BlockSpec((capacity, block), lambda i: (0, i))] * (count - 1),
        out_specs=[
            pl.BlockSpec((rows, block), lambda i: (0, i)),
            pl.BlockSpec((rows, capacity), lambda i: (0, 0)),
        ],
        out_shape=[
            jax.ShapeDtypeStruct((rows, width), F32),
            jax.ShapeDtypeStruct((rows, capacity), BF16),
        ],
        scratch_shapes=[pltpu.VMEM((count - 1, rows, capacity), BF16)],
        compiler_params=params(1, 10),
        cost_estimate=FREE,
        name="combine",
    )(me, meta, *blocks)


def last_sum_kernel(total, pick, block, out):
    out[...] = (total[...] + dot(pick[...], block[...])).astype(BF16)


def last_sum(total, pick, rows):
    tokens, width = total.shape
    block = min(width, 1024)
    return pl.pallas_call(
        last_sum_kernel,
        grid=(width // block,),
        in_specs=[
            pl.BlockSpec((tokens, block), lambda i: (0, i)),
            pl.BlockSpec(pick.shape, lambda i: (0, 0)),
            pl.BlockSpec((rows.shape[0], block), lambda i: (0, i)),
        ],
        out_specs=pl.BlockSpec((tokens, block), lambda i: (0, i)),
        out_shape=jax.ShapeDtypeStruct((tokens, width), BF16),
        compiler_params=params(1, 10),
        cost_estimate=FREE,
        name="last_sum",
    )(total, pick, rows)


def parts_of(capacity, group):
    own = -(-capacity // 128) * 128
    others = -(-(group - 1) * capacity // own) * own
    return own + others, {True: (own, others // own), False: (others, 0)}


def gather_rows(parts, sizes, held):
    at, parts = 0, list(parts)
    for size in sizes:
        mine, parts = parts[:size], parts[size:]
        rows = mine[0][...]
        for other in mine[1:]:
            rows = rows + other[...]
        held[at : at + rows.shape[0], :] = rows
        at += rows.shape[0]
    if at < held.shape[0]:
        held[at:, :] = jnp.zeros((held.shape[0] - at, held.shape[1]), held.dtype)


def part_spec(array, capacity):
    block = (capacity, array.shape[1])
    return pl.BlockSpec(block, lambda i: (0, 0), pipeline_mode=pl.Buffered(buffer_count=1))


def forward_kernel(sizes, *refs):
    count = sum(sizes)
    gate_w, up_w = refs[count : count + 2]
    gate_out, up_out, hidden_out, flipped, held = refs[-5:]

    @pl.when(pl.program_id(0) == 0)
    def _():
        gather_rows(refs[:count], sizes, held)
        step = min(held.shape[1], 256)
        for d in range(0, held.shape[1], step):
            flipped[d : d + step, :] = held[:, d : d + step].T

    gate, up = dot(held[...], gate_w[...]), dot(held[...], up_w[...])
    sigmoid = jax.nn.sigmoid(gate)
    swish = gate * sigmoid
    gate_out[...] = (up * sigmoid * (1.0 + gate * (1.0 - sigmoid))).astype(BF16)
    up_out[...] = swish.astype(BF16)
    hidden_out[...] = (swish * up).T.astype(BF16)


def forward(group, sources, w_pair, before):
    arrays, sizes = sum(sources, []), [len(s) for s in sources]
    capacity, width = min(a.shape[0] for a in arrays), arrays[0].shape[1]
    units = w_pair.shape[1] // 2
    tile = math.gcd(units, 256)
    tiles = units // tile
    total, parts = parts_of(capacity, group)
    rows, part = parts[not before]
    shapes = [
        jax.ShapeDtypeStruct((rows, units), BF16),
        jax.ShapeDtypeStruct((rows, units), BF16),
        jax.ShapeDtypeStruct((units, total), BF16),
        jax.ShapeDtypeStruct((width, total), BF16),
    ]
    first = len(arrays) + 2
    return pl.pallas_call(
        functools.partial(forward_kernel, sizes),
        grid=(tiles,),
        in_specs=[part_spec(a, capacity) for a in arrays]
        + [
            pl.BlockSpec((width, tile), lambda j: (0, j)),
            pl.BlockSpec((width, tile), lambda j: (0, tiles + j)),
        ]
        + [pl.BlockSpec(memory_space=pl.ANY) for _ in before],
        out_specs=[
            pl.BlockSpec((rows, tile), lambda j: (0, j)),
            pl.BlockSpec((rows, tile), lambda j: (0, j)),
            pl.BlockSpec((tile, rows), lambda j: (j, part)),
            pl.BlockSpec((width, rows), lambda j: (0, part)),
        ],
        out_shape=shapes,
        scratch_shapes=[pltpu.VMEM((rows, width), BF16)],
        input_output_aliases={first + i: 2 + i for i in range(len(before))},
        compiler_params=params(1, 20),
        cost_estimate=cost(rows * width * units),
        name="forward",
    )(*arrays, w_pair, w_pair, *before)


def inner_kernel(sizes, rows, tiles, *refs):
    count = sum(sizes)
    down_w, gate_d, up_d, w_ref = refs[count : count + 4]
    last, grads, gate_out, up_out, grad_pre = refs[-5:]
    step = pl.program_id(0)
    units, capacity = grad_pre.shape[1] // 2, last.shape[0]

    @pl.when(step == 0)
    def _():
        gather_rows(refs[:count], sizes, grads)

    for j in range(tiles):

        @pl.when(step == j)
        def _():
            grad_hidden = dot_nt(grads[:rows, :], down_w[...])
            tile = grad_hidden.shape[1]
            for at, slope, out in ((0, gate_d, gate_out), (units, up_d, up_out)):
                value = (grad_hidden * slope[:rows, :].astype(F32)).astype(BF16)
                grad_pre[:, at + j * tile : at + (j + 1) * tile] = value[rows - capacity :, :]
                out[:rows, :] = value
                if rows < out.shape[0]:
                    out[rows:, :] = jnp.zeros((out.shape[0] - rows, tile), BF16)

    @pl.when(step >= tiles)
    def _():
        last[...] = dot_nt(grad_pre[...], w_ref[...]).astype(BF16)


def inner(group, sources, w_down, gate_d, up_d, w_pair, before):
    arrays, sizes = sum(sources, []), [len(s) for s in sources]
    capacity, width = min(a.shape[0] for a in arrays), arrays[0].shape[1]
    units = w_down.shape[0]
    tile = math.gcd(units, 256)
    tiles = units // tile
    block = min(width, 1024)
    total, parts = parts_of(capacity, group)
    held, part = parts[not before]

    def tile_at(i):
        return jnp.minimum(i, tiles - 1)

    def block_at(i):
        return jnp.maximum(i - tiles, 0)

    first = len(arrays) + 4
    return pl.pallas_call(
        functools.partial(inner_kernel, sizes, len(sources) * capacity, tiles),
        grid=(tiles + width // block,),
        in_specs=[part_spec(a, capacity) for a in arrays]
        + [
            pl.BlockSpec((tile, width), lambda i: (tile_at(i), 0)),
            pl.BlockSpec((held, tile), lambda i: (0, tile_at(i))),
            pl.BlockSpec((held, tile), lambda i: (0, tile_at(i))),
            pl.BlockSpec((block, 2 * units), lambda i: (block_at(i), 0)),
        ]
        + [pl.BlockSpec(memory_space=pl.ANY) for _ in before],
        out_specs=[
            pl.BlockSpec((capacity, block), lambda i: (0, block_at(i))),
            pl.BlockSpec((held, width), lambda i: (part, 0)),
            pl.BlockSpec((held, tile), lambda i: (part, tile_at(i))),
            pl.BlockSpec((held, tile), lambda i: (part, tile_at(i))),
        ],
        out_shape=[
            jax.ShapeDtypeStruct((capacity, width), BF16),
            jax.ShapeDtypeStruct((total, width), BF16),
            jax.ShapeDtypeStruct((total, units), BF16),
            jax.ShapeDtypeStruct((total, units), BF16),
        ],
        scratch_shapes=[pltpu.VMEM((capacity, 2 * units), BF16)],
        input_output_aliases={first + i: 1 + i for i in range(len(before))},
        compiler_params=params(1, 20),
        cost_estimate=FREE,
        name="inner",
    )(*arrays, w_down, gate_d, up_d, w_pair, *before)


def back_kernel(sources, gate_ref, up_ref, w_ref, *outs):
    units, capacity = gate_ref.shape[1], outs[0].shape[0]
    rows = sources * capacity
    value = dot_nt(gate_ref[:rows, :], w_ref[:, :units])
    value += dot_nt(up_ref[:rows, :], w_ref[:, units:])
    for m, out in enumerate(outs):
        out[...] = value[m * capacity : (m + 1) * capacity, :].astype(BF16)


def back(group, capacity, gate, up, w_pair):
    width, units = w_pair.shape[0], gate.shape[1]
    held, part = parts_of(capacity, group)[1][False]
    sources = group - 2
    block = min(width, 1024)
    return pl.pallas_call(
        functools.partial(back_kernel, sources),
        grid=(width // block,),
        in_specs=[
            pl.BlockSpec((held, units), lambda i: (part, 0)),
            pl.BlockSpec((held, units), lambda i: (part, 0)),
            pl.BlockSpec((block, 2 * units), lambda i: (i, 0)),
        ],
        out_specs=[pl.BlockSpec((capacity, block), lambda i: (0, i))] * sources,
        out_shape=[jax.ShapeDtypeStruct((capacity, width), BF16)] * sources,
        compiler_params=params(1, 18),
        cost_estimate=FREE,
        name="back",
    )(gate, up, w_pair)


def pair_chunks(flipped_rows, sides, chunk):
    for side in sides:
        for c in range(0, side.shape[1], chunk):
            yield dot(flipped_rows, side[:, c : c + chunk])


def lower_share(rows, chunk):
    return jnp.concatenate([rows[:, c : c + chunk] for c in range(0, rows.shape[1], chunk)], axis=0)


def hold_lower(which, shares, hidden_ref, rows, lower):
    own = hidden_ref.shape[1]
    stacked = jnp.concatenate(
        [hidden_ref[which(r)].astype(F32) for r in range(shares)], axis=0
    ).astype(BF16)
    lower[...] = dot(stacked, rows).reshape(shares, own, rows.shape[1])


def give_kernel(shares, chunk, which_ref, flip_ref, hidden_ref, grads, gate, up, out, lower):
    step = pl.program_id(0)

    @pl.when(step == 0)
    def _():
        hold_lower(lambda r: which_ref[r], shares, hidden_ref, grads[...], lower)

    at = 0
    for piece in pair_chunks(flip_ref[0], (gate[...], up[...]), chunk):
        out[0, at : at + piece.shape[0]] = piece.astype(BF16)
        at += piece.shape[0]
    out[0, at:] = lower_share(lower[step], chunk).astype(BF16)


def shared_operands(flipped, hidden, replicas):
    width, rows = flipped.shape
    units = hidden.shape[0]
    return (
        flipped.reshape(replicas, width // replicas, rows),
        hidden.reshape(replicas, units // replicas, rows),
    )


def give(which, flipped, hidden, grads, gate, up, replicas, chunk):
    rows, width = grads.shape
    units = gate.shape[1]
    shares = replicas // 2
    share_rows = (2 * units * (width // replicas) + (units // replicas) * width) // chunk
    flipped, hidden = shared_operands(flipped, hidden, replicas)
    return pl.pallas_call(
        functools.partial(give_kernel, shares, chunk),
        grid_spec=pltpu.PrefetchScalarGridSpec(
            num_scalar_prefetch=1,
            grid=(shares,),
            in_specs=[pl.BlockSpec((1, width // replicas, rows), lambda i, w: (w[i], 0, 0))]
            + [whole(a) for a in (hidden, grads, gate, up)],
            out_specs=pl.BlockSpec((1, share_rows, chunk), lambda i, w: (i, 0, 0)),
            scratch_shapes=[pltpu.VMEM((shares, units // replicas, width), F32)],
        ),
        out_shape=jax.ShapeDtypeStruct((shares, share_rows, chunk), BF16),
        compiler_params=params(1, 18),
        cost_estimate=FREE,
        name="give",
    )(which, flipped, hidden, grads, gate, up)


def split_kernel(shares, own, came, *outs):
    step = pl.program_id(0)
    total = own[0].astype(F32) + came[0].astype(F32)
    half = total.shape[0] // 2
    for r in range(shares):

        @pl.when(step == r)
        def _():
            outs[2 * r][...] = total[:half].astype(BF16)
            outs[2 * r + 1][...] = total[half:].astype(BF16)


def split(own, came):
    shares, share_rows, chunk = came.shape
    half = share_rows // 2
    share = pl.BlockSpec((1, share_rows, chunk), lambda i: (i, 0, 0))
    halves = pl.pallas_call(
        functools.partial(split_kernel, shares),
        grid=(shares,),
        in_specs=[share, share],
        out_specs=[pl.BlockSpec((half, chunk), lambda i: (0, 0))] * (2 * shares),
        out_shape=[jax.ShapeDtypeStruct((half, chunk), BF16)] * (2 * shares),
        compiler_params=params(1, 18),
        cost_estimate=FREE,
        name="split",
    )(own, came)
    return halves[::2], halves[1::2]


def halvings(shares, bits, before_last):
    terms = {r: [share] for r, share in enumerate(shares)}
    for bit in bits:
        pairs = [(i, i ^ (2 << bit)) for i in range(lax.axis_size("dp"))]
        for r in sorted((r for r in terms if (r >> bit) & 1), reverse=True):
            mine = terms.pop(r)
            if len(mine) > 1:
                mine = [sum(term.astype(F32) for term in mine).astype(BF16)]
            if bit == bits[-1]:
                mine = lax.optimization_barrier((mine[0], before_last))
            terms[r ^ (1 << bit)].append(lax.ppermute(mine[0], "dp", pairs))
    return terms[0]


def finish_kernel(count, chunk, *refs):
    halves, (pair, lower) = (refs[:count], refs[count : 2 * count]), refs[2 * count :]
    totals = []
    for terms in halves:
        total = terms[0][...].astype(F32)
        for term in terms[1:]:
            total += term[...].astype(F32)
        totals.append(total)
    half = totals[0].shape[0]
    at = 0
    for out in (pair, lower):
        rows, columns = out.shape
        for c in range(0, columns, chunk):
            cut = min(max(half - at, 0), rows)
            if cut:
                out[:cut, c : c + chunk] = totals[0][at : at + cut]
            if cut < rows:
                out[cut:, c : c + chunk] = totals[1][at + cut - half : at + rows - half]
            at += rows


def finish(firsts, seconds, pair_shape, lower_shape):
    chunk = firsts[0].shape[1]
    return pl.pallas_call(
        functools.partial(finish_kernel, len(firsts), chunk),
        grid=(1,),
        in_specs=[pl.BlockSpec(a.shape, lambda i: (0, 0)) for a in firsts + seconds],
        out_specs=[
            pl.BlockSpec(pair_shape, lambda i: (0, 0)),
            pl.BlockSpec(lower_shape, lambda i: (0, 0)),
        ],
        out_shape=[
            jax.ShapeDtypeStruct(pair_shape, F32),
            jax.ShapeDtypeStruct(lower_shape, F32),
        ],
        compiler_params=params(1, 24),
        cost_estimate=FREE,
        name="finish",
    )(*firsts, *seconds)


def local(tokens_in, out_grad, expert_ids, gate_weights, w_gate_up, w_down):
    tok_rows, width = tokens_in.shape
    top = expert_ids.shape[1]
    group = lax.axis_size("expert")
    replicas = lax.axis_size("dp")
    units = w_down.shape[1]
    capacity = 5 * tok_rows * top // (4 * group)
    chunk = math.gcd(units, width)
    me = lax.axis_index("expert").astype(jnp.int32)
    replica = lax.axis_index("dp").astype(jnp.int32)
    place = me.reshape(1)
    meta = pieces_of(expert_ids, gate_weights)
    w_pair, w_lower = w_gate_up[0], w_down[0]

    def move(array, pairs):
        return lax.ppermute(array, "expert", pairs)

    def swap(array, m):
        return move(array, [(i, i ^ m) for i in range(group)])

    def after(array, *others):
        return lax.optimization_barrier((array, *others))[0]

    if group == 4 and tok_rows < 2 * capacity:
        far, near, cross = [(0, 2), (3, 1)], [(1, 2), (2, 1)], [(1, 3), (2, 0)]
        far_rows, far_meta = move(tokens_in, far), move(meta, far)
        x0, g0, x1, g1, x2, g2, x3, g3 = pack(
            place, meta, dict(tokens=tokens_in, grads=out_grad), [0, 1, 2, 3], [], capacity, top
        )
        x1, x3, x2 = swap(x1, 1), move(after(x3, far_meta), near), move(x2, cross)
        cx, onward = pack(place, far_meta, dict(tokens=far_rows), [0, 1], [], capacity + 16, top)
        onward = move(onward, [(2, 3), (1, 0)])
        g1 = swap(after(g1, x1), 1)
        g2 = swap(after(g2, x3), 2)
        g3 = swap(after(g3, x2), 3)
        inputs, grads = [[x0], [x1], [cx, x2], [onward, x3]], [[g0], [g1], [g2], [g3]]
    else:
        offsets = list(range(group))
        packed = pack(
            place, meta, dict(tokens=tokens_in, grads=out_grad), offsets, [], capacity, top
        )
        moved = [packed[2 * m : 2 * m + 2] for m in offsets]
        moved = [moved[0]] + [[swap(a, m) for a in moved[m]] for m in offsets[1:]]
        inputs, grads = [[a] for a, _ in moved], [[b] for _, b in moved]

    own_d = forward(group, inputs[:1], w_pair, [])
    others_d = forward(group, inputs[1:], w_pair, own_d[2:])
    own_back, *own_grads = inner(group, grads[:1], w_lower, *own_d[:2], w_pair, [])
    last, *late = inner(group, grads[1:], w_lower, *others_d[:2], w_pair, own_grads)
    returned = [own_back, *back(group, capacity, *late[1:], w_pair), last]
    for m in range(group - 1, 0, -1):
        ahead = returned[m + 1 :] if 2 * m >= group else []
        returned[m] = swap(after(returned[m], *ahead), m)

    shares = replicas // 2
    own = [replica ^ (2 * r) for r in range(shares)]
    operands = (others_d[3], others_d[2], *late)
    first_own = jnp.stack(own) ^ 1
    given = give(first_own, *operands, replicas, chunk)
    came = lax.ppermute(given, "dp", [(i, i ^ 1) for i in range(replicas)])
    mine = give(after(jnp.stack(own), given), *operands, replicas, chunk)
    bits = list(range(shares.bit_length() - 1))
    middle = len(bits) // 2
    first_bits, second_bits = bits, bits[middle:] + bits[:middle]
    first, second = split(mine, came)
    ahead = (returned[1], returned[-1])
    firsts = halvings(first, first_bits, ahead)
    seconds = halvings(second, second_bits, ahead)
    latest = max(1, group // 2)
    offsets = [m for m in range(group) if m != latest] + [latest]
    soon = [returned[m] for m in offsets[:-1]]
    soon, firsts[1], seconds[1] = lax.optimization_barrier((soon, firsts[1], seconds[1]))
    total, pick = combine(place, meta, soon, offsets, top)
    pair_sum, lower_sum = finish(
        firsts, seconds, (width // replicas, 2 * units), (units // replicas, width)
    )
    late_rows, pair_sum, lower_sum, total = lax.optimization_barrier(
        (returned[latest], pair_sum, lower_sum, total)
    )
    grad_tokens = last_sum(total, pick, late_rows)
    return (grad_tokens, pair_sum, lower_sum)


def solution(mesh):
    in_specs = (
        P(("dp", "expert"), None),
        P(("dp", "expert"), None),
        P(("dp", "expert"), None),
        P(("dp", "expert"), None),
        P("expert", None, None),
        P("expert", None, None),
    )
    out_specs = (P(("dp", "expert"), None), P("dp", "expert"), P("dp", "expert"))
    return jax.shard_map(local, mesh=mesh, in_specs=in_specs, out_specs=out_specs, check_vma=False)
```
